32 devices in a mesh: section: 2 (over y), tensor: 2 (over core), dp: 8 (over z, x).
Axes of the slice: x: 2, y: 2, z: 4, core: 2. Of those that a mesh axis runs over, the one named last changes fastest.
Arguments:
- tokens: bfloat16 [16, 282, 1536], P('dp'), may hold values from -6 to 6
- cotangent: bfloat16 [16, 282, 1536], P('dp'), may hold values from -6 to 6
- times: int32 [16], P('dp'), may hold values from 0 to 999
- text_counts: int32 [16], P('dp'), may hold values from 38 to 154, as said below
- time_table: bfloat16 [1000, 1536], replicated, may hold values from -6 to 6
- modulation_weight: bfloat16 [2, 2, 1536, 6, 1536], P('section', None, 'dp', None, 'tensor'), may hold values from -0.15625 to 0.15625
- projection_weight: bfloat16 [2, 2, 1536, 3, 1536], P('section', None, 'dp', None, 'tensor'), may hold values from -0.15625 to 0.15625
- output_weight: bfloat16 [2, 2, 1536, 1536], P('section', None, 'dp', 'tensor'), may hold values from -1.5 to 1.5
- up_weight: bfloat16 [2, 2, 1536, 6144], P('section', None, 'dp', 'tensor'), may hold values from -0.15625 to 0.15625
- down_weight: bfloat16 [2, 2, 1536, 6144], P('section', None, 'dp', 'tensor'), may hold values from -0.078125 to 0.078125
Outputs:
- activations: bfloat16 [2, 16, 282, 1536], P('section', 'dp')
- input_gradient: float32 [2, 16, 282, 1536], P('section', 'dp')
- table_gradient: float32 [1000, 1536], P(None, ('section', 'tensor', 'dp'))
- modulation_gradient: float32 [2, 2, 1536, 6, 1536], P('section', None, 'dp', None, 'tensor')
- projection_gradient: float32 [2, 2, 1536, 3, 1536], P('section', None, 'dp', None, 'tensor')
- output_gradient: float32 [2, 2, 1536, 1536], P('section', None, 'dp', 'tensor')
- up_gradient: float32 [2, 2, 1536, 6144], P('section', None, 'dp', 'tensor')
- down_gradient: float32 [2, 2, 1536, 6144], P('section', None, 'dp', 'tensor')
The draws below stay inside these ranges and needn't reach their ends.
Inputs may be any that keep to these rules, and one draw needn't show every extreme that they name: `text_counts`: some sequence has all 154 text tokens live.
All inputs are finite; a program needn't handle non-finite values.
Results may differ from the reference program's by a relative error of at most 0.03.
Values may be sent and summed in bfloat16 or wider, within the bound.
No kernel may reach another device: no remote copies, remote signals or barrier semaphores. Data moves between devices by JAX's collectives and lax.ppermute only.
A program may use at most 384 MiB of HBM per device.

```python
import jax
import jax.numpy as jnp
from jax import lax

D = 1536
HEADS = 24
HEAD = 64
FF = 6144
IMG = 128
TXT = 154
NSTEPS = 1000
LEN = 282
NSEQ = 16
N_SECTION = 2


def draw_text_counts(key, part):
    first, second = jax.random.split(key)
    counts = jax.random.randint(first, (NSEQ,), TXT // 4, TXT + 1)
    chosen = jax.random.randint(second, (), 0, NSEQ)
    return jnp.where(jnp.arange(NSEQ) == chosen, TXT, counts).astype(jnp.int32)


def plant(entries, rng, low, top_value):
    spot = [jax.random.randint(jax.random.fold_in(rng, axis), (), 0, length) for axis, length in enumerate(entries.shape)]
    longest = entries.shape.index(max(entries.shape))
    beside = spot[:longest] + [(spot[longest] + 1) % entries.shape[longest]] + spot[longest + 1:]
    return entries.at[tuple(spot)].set(low).at[tuple(beside)].set(top_value)


def level_of(own_key, dims, cuts, smallest, high):
    loudness = 1.0
    for axis_at, shards_of in cuts:
        heights = jax.random.uniform(jax.random.fold_in(jax.random.fold_in(own_key, 6), axis_at), (shards_of,), jnp.float32, smallest / len(cuts), high / len(cuts))
        loudness = loudness * jnp.repeat(jnp.exp(heights), dims[axis_at] // shards_of).reshape((-1,) + (1,) * (len(dims) - 1 - axis_at))
    return loudness


def scatter_about(own_key, extent, width, limit, cuts=(), held_as=jnp.bfloat16):
    drawn = width * jax.random.normal(own_key, extent, jnp.float32)
    if cuts:
        drawn = drawn * level_of(own_key, extent, cuts, -0.22, 0.18)
    return jnp.clip(drawn, -limit, limit).astype(held_as)


def setup_inputs(seed: int = 0) -> dict:
    key_list = jax.random.split(jax.random.key(seed), 11)
    return {
        "tokens": scatter_about(key_list[0], (NSEQ, LEN, D), 1.0, 6.0, ((0, 8),)),
        "cotangent": scatter_about(key_list[1], (NSEQ, LEN, D), 1.0, 6.0, ((0, 8),)),
        "times": plant(jax.random.randint(key_list[2], (NSEQ,), 0, NSTEPS), jax.random.fold_in(key_list[2], 1), 0, NSTEPS - 1).astype(jnp.int32),
        "text_counts": draw_text_counts(jax.random.fold_in(key_list[10], 71), 0),
        "time_table": scatter_about(key_list[4], (NSTEPS, D), 1.0, 6.0),
        "modulation_weight": scatter_about(key_list[5], (N_SECTION, 2, D, 6, D), D ** -0.5, 0.15625, ((0, 2), (2, 8), (4, 2))),
        "projection_weight": scatter_about(key_list[6], (N_SECTION, 2, D, 3, D), D ** -0.5, 0.15625, ((0, 2), (2, 8), (4, 2))),
        "output_weight": scatter_about(key_list[7], (N_SECTION, 2, D, D), (D // 96) ** -0.5, 1.5, ((0, 2), (2, 8), (3, 2))),
        "up_weight": scatter_about(key_list[8], (N_SECTION, 2, D, FF), D ** -0.5, 0.15625, ((0, 2), (2, 8), (3, 2))),
        "down_weight": scatter_about(key_list[9], (N_SECTION, 2, D, FF), FF ** -0.5, 0.078125, ((0, 2), (2, 8), (3, 2))),
    }


@jax.custom_vjp
def low(v):
    return lax.optimization_barrier(v.astype(jnp.bfloat16)).astype(jnp.float32)

@jax.custom_vjp
def low_back(v):
    return v

def low_keep(v):
    return (low(v), None)

def low_pass(kept, grad):
    return (grad,)

def back_keep(v):
    return (v, None)

def back_low(kept, grad):
    return (low(grad),)
low.defvjp(low_keep, low_pass)
low_back.defvjp(back_keep, back_low)
HIGH = lax.Precision.HIGHEST

def norm_rows(values):
    centre = lax.optimization_barrier(jnp.mean(values, axis=-1, keepdims=True))
    spread = values - centre
    variance = lax.optimization_barrier(jnp.mean(spread * spread, axis=-1, keepdims=True))
    return spread * lax.rsqrt(variance + 1e-06)

def gelu_tanh(values):
    inner = 0.7978845608028654 * (values + 0.044715 * values * values * values)
    return 0.5 * values * (1.0 + jnp.tanh(inner))

def layer(layer_in, scaled, count, mod_w, proj_w, out_w, up_w, down_w):
    sides = (layer_in[:IMG], layer_in[IMG:])
    adapts = []
    pieces = []
    for side in range(2):
        adapt = low_back(jnp.einsum('d,dkc->kc', scaled, mod_w[side], precision=HIGH))
        normed = low(norm_rows(sides[side]) * (1.0 + adapt[1]) + adapt[0])
        packed = low(low_back(jnp.einsum('td,dkc->tkc', normed, proj_w[side], precision=HIGH)))
        adapts.append(adapt)
        pieces.append(packed)
    packed = jnp.concatenate(pieces, 0).reshape(LEN, 3, HEADS, HEAD)
    scores = jnp.einsum('qhd,khd->hqk', packed[:, 0], packed[:, 1], precision=HIGH) * HEAD ** (-0.5)
    live = jnp.arange(LEN) < IMG + count
    scores = low_back(jnp.where(live[None, None, :], scores, -1e+30))
    probs = low(jax.nn.softmax(scores, axis=-1))
    mixed = jnp.einsum('hqk,khd->qhd', probs, packed[:, 2], precision=HIGH).reshape(LEN, D)
    mixed = low(low_back(mixed))
    mixes = (mixed[:IMG], mixed[IMG:])
    results = []
    for side in range(2):
        adapt = adapts[side]
        branch = low_back(jnp.einsum('tc,oc->to', mixes[side], out_w[side], precision=HIGH))
        middle = sides[side] + adapt[2] * branch
        second = low(norm_rows(middle) * (1.0 + adapt[4]) + adapt[3])
        before = low_back(jnp.einsum('td,df->tf', second, up_w[side], precision=HIGH))
        after = low(gelu_tanh(before))
        feed = low_back(jnp.einsum('tf,of->to', after, down_w[side], precision=HIGH))
        results.append(middle + adapt[5] * feed)
    return jnp.concatenate(results, 0)

def reference(tokens, cotangent, times, text_counts, time_table, modulation_weight, projection_weight, output_weight, up_weight, down_weight):
    probes = jnp.zeros((N_SECTION, NSEQ, LEN, D), jnp.float32)

    def forward(inputs, probe, table, mod_w, proj_w, out_w, up_w, down_w):

        def one(item):
            seq_in, seq_probe, seq_time, seq_count = item
            scaled = low(jax.nn.silu(table[seq_time]))
            current = seq_in + seq_probe[0]
            outputs = []
            for layer_num in range(N_SECTION):
                result = layer(current, scaled, seq_count, mod_w[layer_num], proj_w[layer_num], out_w[layer_num], up_w[layer_num], down_w[layer_num])
                leaving = low(low_back(result))
                outputs.append(leaving)
                if layer_num + 1 < N_SECTION:
                    current = leaving + seq_probe[layer_num + 1]
            return jnp.stack(outputs)
        return lax.map(jax.checkpoint(one), (inputs, jnp.swapaxes(probe, 0, 1), times, text_counts))
    operands = (tokens.astype(jnp.float32), probes, time_table.astype(jnp.float32), modulation_weight.astype(jnp.float32), projection_weight.astype(jnp.float32), output_weight.astype(jnp.float32), up_weight.astype(jnp.float32), down_weight.astype(jnp.float32))
    outputs, pull = jax.vjp(forward, *operands)
    top_grads = jnp.zeros_like(outputs).at[:, N_SECTION - 1].set(cotangent.astype(jnp.float32))
    grads = pull(top_grads)
    activations = jnp.swapaxes(outputs, 0, 1).astype(jnp.bfloat16)
    return (activations, grads[1], grads[2], grads[3], grads[4], grads[5], grads[6], grads[7])
```

```python
import jax
import jax.numpy as jnp
from jax import lax
from jax.sharding import PartitionSpec as P

HEAD = 64
IMG = 128
BOX = 8


def norm_rows(values):
    centre = jnp.mean(values, axis=-1, keepdims=True)
    spread = values - centre
    variance = jnp.mean(spread * spread, axis=-1, keepdims=True)
    return spread * lax.rsqrt(variance + 1e-06)


def modulate(values, scale, shift):
    return norm_rows(values) * (1.0 + scale[:, None]) + shift[:, None]


def gelu_tanh(values):
    inner = 0.7978845608028654 * (values + 0.044715 * values * values * values)
    return 0.5 * values * (1.0 + jnp.tanh(inner))


def silu_slope(values):
    sigma = jax.nn.sigmoid(values)
    return sigma * (1.0 + values * (1.0 - sigma))


def left_dot(left, weight):
    return lax.dot_general(
        left, weight, (((1,), (0,)), ((), ())), preferred_element_type=jnp.float32
    )


def right_dot(left, weight):
    return lax.dot_general(
        left, weight, (((1,), (1,)), ((), ())), preferred_element_type=jnp.float32
    )


def rows_dot(left, right):
    return lax.dot_general(
        left, right, (((0,), (0,)), ((), ())), preferred_element_type=jnp.float32
    )


def flat(leaf):
    return leaf.reshape(-1, leaf.shape[-1])


def low(leaf):
    return leaf.astype(jnp.bfloat16)


def wide(leaf):
    return leaf.astype(jnp.float32)


def on_device(
    tokens,
    cotangent,
    times,
    text_counts,
    time_table,
    modulation_weight,
    projection_weight,
    output_weight,
    up_weight,
    down_weight,
):
    micro, length, width = tokens.shape
    sections = lax.axis_size("section")
    section = lax.axis_index("section")
    parts = lax.axis_size("tensor")
    part = lax.axis_index("tensor")
    ranks = lax.axis_size("dp")
    rank = lax.axis_index("dp")
    local_width = projection_weight.shape[4]
    heads_local = local_width // HEAD
    rows = projection_weight.shape[2]
    scale = HEAD ** (-0.5)

    inner = [r for r in range(ranks) if (r >> 1) % 4 in (1, 2)]
    outer = [r for r in range(ranks) if (r >> 1) % 4 in (0, 3)]
    is_inner = jnp.logical_or((rank >> 1) % 4 == 1, (rank >> 1) % 4 == 2)
    pair_all = [(r, r ^ 1) for r in range(ranks)]
    pair_inner = [(r, r ^ 1) for r in inner]
    pair_outer = [(r, r ^ 1) for r in outer]
    inward = [(r, r ^ 2) for r in outer]
    outward = [(r, r ^ 2) for r in inner]
    across = [(r, r ^ 6) for r in inner]
    boxes = ranks // BOX
    box_groups = [[b * BOX + i for b in range(boxes)] for i in range(BOX)]

    def hop(value, pairs):
        return lax.ppermute(value, "dp", pairs)

    def swap(value):
        return lax.ppermute(value, "tensor", [(p, p ^ 1) for p in range(parts)])

    def along(value, steps):
        first, last = (max(0, -steps), min(sections, sections - steps))
        return lax.ppermute(value, "section", [(s, s + steps) for s in range(first, last)])

    def place(step):
        return ((rank ^ step) % BOX) * rows

    def gather(own, pair_heavy):
        pieces = {0: own}
        pieces[1] = hop(own, pair_all)
        pieces[2] = hop(own, inward)
        pieces[6] = hop(own, across)
        pieces[3] = hop(pieces[1], inward)
        pieces[4] = hop(pieces[2], across)
        pieces[7] = hop(pieces[6], pair_inner) if pair_heavy else hop(pieces[1], across)
        pieces[5] = hop(pieces[4], pair_inner)
        whole = jnp.zeros((own.shape[0], BOX * rows, own.shape[2]), own.dtype)
        for step, piece in pieces.items():
            whole = lax.dynamic_update_slice_in_dim(whole, piece, place(step), 1)
        if boxes > 1:
            whole = lax.all_gather(whole, "dp", axis=1, tiled=True, axis_index_groups=box_groups)
        return whole

    def scatter(whole, pair_heavy):
        if boxes > 1:
            whole = lax.psum_scatter(
                whole, "dp", scatter_dimension=1, tiled=True, axis_index_groups=box_groups
            )

        def block(step):
            return wide(lax.dynamic_slice_in_dim(whole, place(step), rows, 1))

        far = low(block(4) + wide(hop(low(block(5)), pair_inner)))
        if pair_heavy:
            near = low(block(6) + wide(hop(low(block(7)), pair_inner)))
            to_end = wide(hop(far, across))
            mine = wide(hop(near, across))
            beside = wide(hop(low(block(1)), pair_inner))
        else:
            to_end = wide(hop(far, across))
            mine = wide(hop(low(block(6)), across))
            theirs = wide(hop(low(block(7)), across))
            beside = wide(hop(low(block(1) + theirs), pair_inner))
        inner_sum = block(0) + mine + beside
        end_sum = wide(hop(low(block(2) + to_end), outward))
        end_pair = wide(hop(hop(low(block(3)), outward), pair_outer))
        return jnp.where(is_inner, inner_sum, end_sum + end_pair)

    def two_core(pairs):
        return [(ranks + source, ranks + target) for source, target in pairs]

    def take_in(value):
        moved = lax.ppermute(value, ("tensor", "dp"), two_core(inward))
        return jnp.where(part == 0, value, moved)

    def hand_back(value):
        moved = lax.ppermute(value, ("tensor", "dp"), two_core(outward))
        held = jnp.where(is_inner, value, moved)
        return jnp.where((part == 0) == is_inner, held, swap(held))

    own_rank = rank ^ (2 * part)
    other_rank = rank ^ (2 * (1 - part))
    sequences = take_in(tokens)
    triple_matrix = gather(projection_weight[0].reshape(2, rows, 3 * local_width), False)
    out_matrix = gather(output_weight[0], True)
    up_matrix = gather(up_weight[0], True)
    down_matrix = gather(down_weight[0], False)
    top_grad = take_in(cotangent)

    times_all = lax.all_gather(times, "dp", axis=0, tiled=True)
    counts_all = lax.all_gather(text_counts, "dp", axis=0, tiled=True)
    onehot_all = (times_all[:, None] == jnp.arange(time_table.shape[0])[None, :]).astype(
        jnp.bfloat16
    )
    cond_all = jnp.dot(onehot_all, time_table, preferred_element_type=jnp.float32)
    cond_rows = lax.dynamic_slice_in_dim(cond_all, rank * rows, rows, 1)
    scaled_rows = jax.nn.silu(cond_rows).astype(jnp.bfloat16)
    adapt_part = jnp.einsum(
        "nd,sdkc->nskc", scaled_rows, modulation_weight[0], preferred_element_type=jnp.float32
    )
    adapt_all = lax.psum(adapt_part, "dp")

    def of_rank(stacked, index):
        return lax.dynamic_slice_in_dim(stacked, index * micro, micro, 0)

    def joined(mine, theirs, axis):
        return jnp.where(
            part == 0,
            jnp.concatenate([mine, theirs], axis),
            jnp.concatenate([theirs, mine], axis),
        )

    adapt_mine = of_rank(adapt_all, own_rank)
    adapt = joined(adapt_mine, swap(of_rank(adapt_all, other_rank)), 3)
    counts = jnp.concatenate([of_rank(counts_all, own_rank), of_rank(counts_all, other_rank)])
    live = jnp.arange(length)[None, :] < IMG + counts[:, None]
    group = parts * micro

    def both(own):
        return jnp.concatenate([own, swap(own)], 0)

    def own_total(partial, own_like):
        partial = low(partial).reshape(group, -1, width)
        return wide(partial[:micro]) + wide(swap(partial[micro:]))

    def split(leaf):
        return (leaf[:, :IMG], leaf[:, IMG:])

    def attend(queries, key_rows):
        scores = (
            jnp.einsum("nqhd,nkhd->nhqk", queries, key_rows, preferred_element_type=jnp.float32)
            * scale
        )
        return jnp.where(live[:, None, None, :], scores, -1e30)

    def layer_forward(sides):
        normed, pieces = ([], [])
        for side in range(2):
            first = both(low(modulate(wide(sides[side]), adapt[:, side, 1], adapt[:, side, 0])))
            normed.append(flat(first))
            packed = low(left_dot(normed[side], triple_matrix[side]))
            pieces.append(packed.reshape(group, -1, 3, heads_local, HEAD))
        packed = jnp.concatenate(pieces, 1)
        scores = attend(packed[:, :, 0], packed[:, :, 1])
        totals = jax.nn.logsumexp(scores, axis=-1)
        probability = low(jnp.exp(scores - totals[..., None]))
        mixed = jnp.einsum(
            "nhqk,nkhd->nqhd", probability, packed[:, :, 2], preferred_element_type=jnp.float32
        )
        mixes = [flat(m) for m in split(low(mixed).reshape(group, length, local_width))]
        kept = {"sides": sides, "normed": normed, "packed": packed, "totals": totals}
        kept.update(mixes=mixes, branch=[], middles=[], seconds=[], befores=[], afters=[], feed=[])
        results = []
        for side in range(2):
            branch = own_total(right_dot(mixes[side], out_matrix[side]), sides[side])
            middle = wide(sides[side]) + adapt[:, side, 2][:, None] * branch
            second = flat(both(low(modulate(middle, adapt[:, side, 4], adapt[:, side, 3]))))
            before = left_dot(second, up_matrix[side])
            after = low(gelu_tanh(before))
            feed = own_total(right_dot(after, down_matrix[side]), sides[side])
            results.append(low(middle + adapt[:, side, 5][:, None] * feed))
            kept["branch"].append(branch)
            kept["middles"].append(middle)
            kept["seconds"].append(second)
            kept["befores"].append(before)
            kept["afters"].append(after)
            kept["feed"].append(feed)
        return (results, kept)

    def layer_backward(incoming, kept):
        feed_grads, up_grads, middle_grads, branch_grads, mix_grads = ([], [], [], [], [])
        vectors = [[None] * 6, [None] * 6]
        for side in range(2):
            upstream = wide(incoming[side])
            feed_grad = flat(both(low(upstream * adapt[:, side, 5][:, None])))
            vectors[side][5] = jnp.sum(upstream * kept["feed"][side], axis=1)
            after_grad = left_dot(feed_grad, down_matrix[side])
            unused, gelu_back = jax.vjp(gelu_tanh, kept["befores"][side])
            up_grad = low(gelu_back(after_grad)[0])
            feed_grads.append(feed_grad)
            up_grads.append(up_grad)
            second_grad = own_total(right_dot(up_grad, up_matrix[side]), upstream)
            unused, norm_back = jax.vjp(
                modulate, kept["middles"][side], adapt[:, side, 4], adapt[:, side, 3]
            )
            middle_part, vectors[side][4], vectors[side][3] = norm_back(second_grad)
            middle_grad = upstream + middle_part
            branch_grad = flat(both(low(middle_grad * adapt[:, side, 2][:, None])))
            middle_grads.append(middle_grad)
            branch_grads.append(branch_grad)
            vectors[side][2] = jnp.sum(middle_grad * kept["branch"][side], axis=1)
            mix_grad = low(left_dot(branch_grad, out_matrix[side]))
            mix_grads.append(mix_grad.reshape(group, -1, heads_local, HEAD))
        mix_grad = jnp.concatenate(mix_grads, 1)
        packed = kept["packed"]
        scores = attend(packed[:, :, 0], packed[:, :, 1])
        soft = jnp.exp(scores - kept["totals"][..., None])
        prob_grad = jnp.einsum(
            "nqhd,nkhd->nhqk", mix_grad, packed[:, :, 2], preferred_element_type=jnp.float32
        )
        score_grad = low(soft * (prob_grad - jnp.sum(prob_grad * soft, axis=-1, keepdims=True)))
        query_grad = (
            jnp.einsum(
                "nhqk,nkhd->nqhd", score_grad, packed[:, :, 1], preferred_element_type=jnp.float32
            )
            * scale
        )
        key_grad = (
            jnp.einsum(
                "nhqk,nqhd->nkhd", score_grad, packed[:, :, 0], preferred_element_type=jnp.float32
            )
            * scale
        )
        value_grad = jnp.einsum(
            "nhqk,nqhd->nkhd", low(soft), mix_grad, preferred_element_type=jnp.float32
        )
        triple_grad = low(jnp.stack([query_grad, key_grad, value_grad], axis=2))
        triples = [flat(t) for t in split(triple_grad.reshape(group, length, 3 * local_width))]
        results = []
        for side in range(2):
            layer_in = wide(kept["sides"][side])
            first_grad = own_total(right_dot(triples[side], triple_matrix[side]), layer_in)
            unused, norm_back = jax.vjp(modulate, layer_in, adapt[:, side, 1], adapt[:, side, 0])
            input_part, vectors[side][1], vectors[side][0] = norm_back(first_grad)
            results.append(middle_grads[side] + input_part)
        vectors = jnp.stack([jnp.stack(v, 1) for v in vectors], 1)
        return (results, vectors, triples, branch_grads, up_grads, feed_grads)

    first_in = split(sequences)
    entering = first_in
    for phase in range(sections):
        if phase:
            received = [along(leaf, 1) for leaf in leaving]
            entering = [
                jnp.where(section == 0, leaf, moved) for leaf, moved in zip(first_in, received)
            ]
        leaving, kept = layer_forward(entering)
    last_grad = split(top_grad)
    upstream = last_grad
    for phase in range(sections):
        if phase:
            received = [along(low(leaf), -1) for leaf in input_grads]
            upstream = [
                jnp.where(section == sections - 1, leaf, moved)
                for leaf, moved in zip(last_grad, received)
            ]
        input_grads, vectors, triples, branch_grads, up_grads, feed_grads = layer_backward(
            upstream, kept
        )
    activations = hand_back(jnp.concatenate(leaving, 1))[None]

    def weight_grad(lefts, rights):
        return jnp.stack([low(rows_dot(left, right)) for left, right in zip(lefts, rights)])

    down_gradient = scatter(weight_grad(feed_grads, kept["afters"]), False)[None]
    up_gradient = scatter(weight_grad(kept["seconds"], up_grads), True)[None]
    output_gradient = scatter(weight_grad(branch_grads, kept["mixes"]), True)[None]
    projection_gradient = scatter(weight_grad(kept["normed"], triples), False)
    projection_gradient = projection_gradient.reshape(2, rows, 3, local_width)[None]
    input_gradient = hand_back(jnp.concatenate(input_grads, 1))[None]

    vectors = low(vectors)
    halves = (vectors[..., :local_width], vectors[..., local_width:])
    mine = jnp.where(part == 0, halves[0], halves[1])
    theirs = swap(jnp.where(part == 0, halves[1], halves[0]))
    cores = jnp.where(part == 0, jnp.stack([mine, theirs]), jnp.stack([theirs, mine]))
    every = lax.all_gather(cores, "dp", axis=0, tiled=False)
    adapt_every = jnp.concatenate(
        [every[r, 0] if r in inner else every[r ^ 2, 1] for r in range(ranks)], 0
    )
    modulation_gradient = jnp.einsum(
        "nr,nskc->srkc", scaled_rows, adapt_every, preferred_element_type=jnp.float32
    )[None]
    cond_rows_grad = jnp.einsum(
        "nskc,sdkc->nd", adapt_every, modulation_weight[0], preferred_element_type=jnp.float32
    )
    cond_rows_grad = silu_slope(cond_rows) * lax.psum(cond_rows_grad, ("section", "tensor"))
    cond_grad = lax.all_gather(cond_rows_grad, "dp", axis=1, tiled=True)
    columns = width // (sections * parts * ranks)
    first_column = ((section * parts + part) * ranks + rank) * columns
    table_gradient = jnp.dot(
        wide(onehot_all).T,
        lax.dynamic_slice_in_dim(cond_grad, first_column, columns, 1),
        precision=lax.Precision.HIGHEST,
    )
    return (
        activations,
        input_gradient,
        table_gradient,
        modulation_gradient,
        projection_gradient,
        output_gradient,
        up_gradient,
        down_gradient,
    )


def solution(mesh):
    in_specs = (
        P("dp", None, None),
        P("dp", None, None),
        P("dp"),
        P("dp"),
        P(),
        P("section", None, "dp", None, "tensor"),
        P("section", None, "dp", None, "tensor"),
        P("section", None, "dp", "tensor"),
        P("section", None, "dp", "tensor"),
        P("section", None, "dp", "tensor"),
    )
    out_specs = (
        P("section", "dp", None, None),
        P("section", "dp", None, None),
        P(None, ("section", "tensor", "dp")),
        P("section", None, "dp", None, "tensor"),
        P("section", None, "dp", None, "tensor"),
        P("section", None, "dp", "tensor"),
        P("section", None, "dp", "tensor"),
        P("section", None, "dp", "tensor"),
    )
    return jax.shard_map(
        on_device, mesh=mesh, in_specs=in_specs, out_specs=out_specs, check_vma=False
    )
```

```python
import functools
from types import SimpleNamespace

import jax
import jax.numpy as jnp
from jax import lax
from jax.experimental import pallas as pl
from jax.experimental.pallas import tpu as pltpu
from jax.sharding import PartitionSpec as P

HEAD = 64
IMG = 128
BOX = 8
(FAR_PAIR, NEAR_PAIR, END, MINE, THEIRS, BESIDE, END_SUM, END_PAIR, CROSSED) = range(100, 109)
(PAIR_IN, END_IN, ACROSS_IN, PAIR_LINK, END_LINK, ACROSS_LINK, ENDED) = range(109, 116)
VMEM_LIMIT = 40 * 1024 * 1024


def norm_rows(values):
    centre = jnp.mean(values, axis=-1, keepdims=True)
    spread = values - centre
    variance = jnp.mean(spread * spread, axis=-1, keepdims=True)
    return spread * lax.rsqrt(variance + 1e-06)


def gelu_tanh(values):
    inner = 0.7978845608028654 * (values + 0.044715 * values * values * values)
    return 0.5 * values * (1.0 + jnp.tanh(inner))


def gelu_slope(values):
    square = values * values
    bend = jnp.tanh(0.7978845608028654 * (values + 0.044715 * values * square))
    return 0.5 * (1.0 + bend) + 0.5 * values * (1.0 - bend * bend) * (
        0.7978845608028654 * (1.0 + 0.134145 * square)
    )


def silu_slope(values):
    sigma = jax.nn.sigmoid(values)
    return sigma * (1.0 + values * (1.0 - sigma))


def left_dot(left, weight):
    return lax.dot_general(
        left, weight, (((1,), (0,)), ((), ())), preferred_element_type=jnp.float32
    )


def right_dot(left, weight):
    return lax.dot_general(
        left, weight, (((1,), (1,)), ((), ())), preferred_element_type=jnp.float32
    )


def rows_dot(left, right):
    return lax.dot_general(
        left, right, (((0,), (0,)), ((), ())), preferred_element_type=jnp.float32
    )


def flat(leaf):
    return leaf.reshape(-1, leaf.shape[-1])


def low(leaf):
    return leaf.astype(jnp.bfloat16)


def wide(leaf):
    return leaf.astype(jnp.float32)


def pair_mask(rows, half):
    lanes = lax.broadcasted_iota(jnp.int32, (rows, 2 * HEAD), 1)
    return lanes < HEAD if half == 0 else lanes >= HEAD


def only_half(leaf, half):
    return jnp.where(pair_mask(leaf.shape[0], half), leaf, jnp.zeros_like(leaf))


def stacked_rows(refs, column):
    lanes = pl.ds(column, 2 * HEAD)
    return jnp.concatenate([ref[:, lanes] for ref in refs], 0)


def put_rows(refs, column, value):
    start = 0
    for ref in refs:
        stop = start + ref.shape[0]
        ref[:, pl.ds(column, 2 * HEAD)] = value[start:stop]
        start = stop


def attention_kernel(counts, image, text, mixed_image, mixed_text):
    width = mixed_image.shape[1]
    total = image.shape[0] + text.shape[0]
    bound = IMG + counts[pl.program_id(0)]
    live = lax.broadcasted_iota(jnp.int32, (2 * total, total), 1) < bound
    for column in range(0, width, 2 * HEAD):
        queries = stacked_rows((image, text), column) * HEAD ** (-0.5)
        keys = stacked_rows((image, text), width + column)
        values = stacked_rows((image, text), 2 * width + column)
        asked = jnp.concatenate([only_half(queries, half) for half in range(2)], 0)
        scores = jnp.where(live, right_dot(asked, keys), -1e30)
        weights = jnp.exp(scores - jnp.max(scores, axis=-1, keepdims=True))
        share = 1.0 / jnp.sum(weights, axis=-1, keepdims=True)
        mixed = left_dot(low(weights), values) * share
        mixed = low(jnp.where(pair_mask(total, 0), mixed[:total], mixed[total:]))
        put_rows((mixed_image, mixed_text), column, mixed)


def attention_back_kernel(
    counts, image, text, grad_image, grad_text, out_image, out_text
):
    width = grad_image.shape[1]
    total = image.shape[0] + text.shape[0]
    bound = IMG + counts[pl.program_id(0)]
    live = lax.broadcasted_iota(jnp.int32, (total, 2 * total), 0) < bound
    scale = HEAD ** (-0.5)
    for column in range(0, width, 2 * HEAD):
        queries = stacked_rows((image, text), column) * scale
        keys = stacked_rows((image, text), width + column)
        values = stacked_rows((image, text), 2 * width + column)
        grads = stacked_rows((grad_image, grad_text), column)
        asked = jnp.concatenate([only_half(queries, half) for half in range(2)], 0)
        given = jnp.concatenate([only_half(grads, half) for half in range(2)], 0)
        scores = jnp.where(live, right_dot(keys, asked), -1e30)
        soft = jnp.exp(scores - jnp.max(scores, axis=0, keepdims=True))
        soft = soft * (1.0 / jnp.sum(soft, axis=0, keepdims=True))
        prob_grad = right_dot(values, given)
        drop = jnp.sum(prob_grad * soft, axis=0, keepdims=True)
        score_grad = low(soft * (prob_grad - drop))
        query_grad = rows_dot(score_grad, keys) * scale
        query_grad = jnp.where(pair_mask(total, 0), query_grad[:total], query_grad[total:])
        refs = (out_image, out_text)
        put_rows(refs, column, low(query_grad))
        put_rows(refs, width + column, low(left_dot(score_grad, asked)))
        put_rows(refs, 2 * width + column, low(left_dot(low(soft), given)))


def by_sequence_call(kernel, counts, inputs, widths, name, matmuls, light):
    group = counts.shape[0]

    def spec(rows, width):
        return pl.BlockSpec((rows, width), lambda n, counts: (n, 0))

    rows = [leaf.shape[0] // group for leaf in inputs[:2]]
    total = sum(rows)
    return pl.pallas_call(
        kernel,
        grid_spec=pltpu.PrefetchScalarGridSpec(
            num_scalar_prefetch=1,
            grid=(group,),
            in_specs=[spec(leaf.shape[0] // group, leaf.shape[1]) for leaf in inputs],
            out_specs=[spec(count, widths) for count in rows],
        ),
        out_shape=[
            jax.ShapeDtypeStruct((group * count, widths), jnp.bfloat16) for count in rows
        ],
        compiler_params=pltpu.CompilerParams(vmem_limit_bytes=48 * 1024 * 1024),
        cost_estimate=estimate(
            7 * matmuls * group * total * total * 12 * 2 * HEAD,
            sum(leaf.size for leaf in inputs) + group * total * widths,
            light,
        ),
        name=name,
    )(counts, *inputs)


def attention(counts, packed, heads):
    return by_sequence_call(
        attention_kernel, counts, list(packed), heads * HEAD, "attention", 2, False
    )


def attention_back(counts, packed, grads, heads, light):
    return by_sequence_call(
        attention_back_kernel,
        counts,
        list(packed) + list(grads),
        3 * heads * HEAD,
        "attention_back",
        5,
        light,
    )


def joined_rows(refs):
    values = [ref[...] for ref in refs]
    return values[0] if len(values) == 1 else jnp.concatenate(values, 0)


def store_rows(refs, value):
    start = 0
    for ref in refs:
        stop = start + ref.shape[0]
        ref[...] = value[start:stop].astype(ref.dtype)
        start = stop


def product_kernel(counts, dims, finish, *refs):
    lefts, extras, outs = counts
    right = refs[lefts][...]
    total = lax.dot_general(
        joined_rows(refs[:lefts]), right, (dims, ((), ())), preferred_element_type=jnp.float32
    )
    refs = refs[lefts + 1 :]
    results = finish(total, *[ref[...] for ref in refs[:extras]])
    refs = refs[extras:]
    for count, value in zip(outs, results):
        store_rows(refs[:count], value)
        refs = refs[count:]


def turned_kernel(lefts, tiles, *refs):
    turned = refs[-len(lefts) :]
    result = refs[-len(lefts) - 1]
    step = pl.program_id(0)
    start = 0
    for side, count in enumerate(lefts):
        sources = refs[start : start + count]
        right = refs[start + count]
        start += count + 1

        @pl.when(step == side * tiles)
        def _(sources=sources, held=turned[side]):
            held[...] = joined_rows(sources).T

        @pl.when(jnp.logical_and(step >= side * tiles, step < (side + 1) * tiles))
        def _(right=right, held=turned[side]):
            result[...] = low(left_dot(held[...], right[...]))


def estimate(flops, values, light):
    return pl.CostEstimate(flops=2 * flops, bytes_accessed=2 * values, transcendentals=0)


def product(lefts, right, side, turned, tile, outs, light, finish=None, extras=()):
    depth = lefts[0].shape[1]
    width = right.shape[1] if turned else right.shape[2]
    if turned:
        right_spec = pl.BlockSpec((None, tile, depth), lambda n: (side, n, 0))
    else:
        right_spec = pl.BlockSpec((None, depth, tile), lambda n: (side, 0, n))
    rows = sum(leaf.shape[0] for leaf in lefts)
    counts = [count for group in outs for count in group]
    kernel = functools.partial(
        product_kernel,
        (len(lefts), len(extras), [len(group) for group in outs]),
        ((1,), (1 if turned else 0,)),
        finish or (lambda total: (total,)),
    )
    return pl.pallas_call(
        kernel,
        grid=(width // tile,),
        in_specs=[pl.BlockSpec(leaf.shape, lambda n: (0, 0)) for leaf in lefts]
        + [right_spec]
        + [pl.BlockSpec((rows, tile), lambda n: (0, n)) for leaf in extras],
        out_specs=[pl.BlockSpec((count, tile), lambda n: (0, n)) for count in counts],
        out_shape=[jax.ShapeDtypeStruct((count, width), jnp.bfloat16) for count in counts],
        compiler_params=pltpu.CompilerParams(vmem_limit_bytes=VMEM_LIMIT),
        cost_estimate=estimate(2 * rows * depth * width, depth * width + 2 * rows * width, light),
    )(*lefts, right, *extras)


def turned_product(lefts, rights, tile, light):
    depth, width = lefts[0][0].shape[1], rights[0].shape[1]
    tiles = width // tile
    in_specs, operands, scratch = ([], [], [])
    for side, (left, right) in enumerate(zip(lefts, rights)):
        first = side * tiles
        in_specs += [pl.BlockSpec(leaf.shape, lambda n: (0, 0)) for leaf in left]
        in_specs.append(
            pl.BlockSpec(
                (right.shape[0], tile), lambda n, first=first: (0, jnp.clip(n - first, 0, tiles - 1))
            )
        )
        operands += list(left) + [right]
        scratch.append(pltpu.VMEM((depth, right.shape[0]), jnp.bfloat16))
    rows = sum(right.shape[0] for right in rights)
    return pl.pallas_call(
        functools.partial(turned_kernel, [len(left) for left in lefts], tiles),
        grid=(len(lefts) * tiles,),
        in_specs=in_specs,
        out_specs=pl.BlockSpec((None, depth, tile), lambda n: (n // tiles, 0, n % tiles)),
        out_shape=jax.ShapeDtypeStruct((len(lefts), depth, width), jnp.bfloat16),
        scratch_shapes=scratch,
        compiler_params=pltpu.CompilerParams(vmem_limit_bytes=VMEM_LIMIT),
        cost_estimate=estimate(2 * rows * depth * width, depth * width, light),
    )(*operands)


def with_gelu(before):
    return before, gelu_tanh(before)


def times_slope(after_grad, before):
    return (after_grad * gelu_slope(wide(before)),)


def on_device(
    tokens,
    cotangent,
    times,
    text_counts,
    time_table,
    modulation_weight,
    projection_weight,
    output_weight,
    up_weight,
    down_weight,
):
    micro, length, width = tokens.shape
    sections = lax.axis_size("section")
    section = lax.axis_index("section")
    parts = lax.axis_size("tensor")
    part = lax.axis_index("tensor")
    ranks = lax.axis_size("dp")
    rank = lax.axis_index("dp")
    local_width = projection_weight.shape[4]
    rows = projection_weight.shape[2]

    inner = [r for r in range(ranks) if (r >> 1) % 4 in (1, 2)]
    outer = [r for r in range(ranks) if (r >> 1) % 4 in (0, 3)]
    is_inner = jnp.logical_or((rank >> 1) % 4 == 1, (rank >> 1) % 4 == 2)
    pair_all = [(r, r ^ 1) for r in range(ranks)]
    pair_inner = [(r, r ^ 1) for r in inner]
    pair_outer = [(r, r ^ 1) for r in outer]
    inward = [(r, r ^ 2) for r in outer]
    outward = [(r, r ^ 2) for r in inner]
    across = [(r, r ^ 6) for r in inner]
    boxes = ranks // BOX
    box_groups = [[b * BOX + i for b in range(boxes)] for i in range(BOX)]

    links = {}
    depths = {}

    def tied(value, holder, name):
        value, holder[name] = lax.optimization_barrier((value, holder[name]))
        return value

    def hop(value, pairs, link=None, holder=None, name=0, axis="dp"):
        queue = links.setdefault(link, [])
        depth = depths.get(link, 1)
        if link is not None and len(queue) >= depth:
            value = tied(value, *queue[-depth])
        moved = lax.ppermute(value, axis, pairs)
        holder = {} if holder is None else holder
        holder[name] = moved
        if link is not None:
            queue.append((holder, name))
        return moved

    def by_bits(bit):
        return [(r, r ^ bit) for r in range(ranks)]

    def spread_small(value, axis, queued=False, gates=()):
        bit = 1
        gates = list(gates)
        while bit < ranks:
            link = {1: PAIR_LINK, 2: END_LINK, 4: ACROSS_LINK}.get(bit) if queued else None
            if bit > 1 and gates:
                value, _ = lax.optimization_barrier((value, gates.pop(0)))
            other = hop(value, by_bits(bit), link)
            value = jnp.where(
                (rank & bit) == 0,
                jnp.concatenate([value, other], axis),
                jnp.concatenate([other, value], axis),
            )
            bit *= 2
        return value

    def swap(value):
        return lax.ppermute(value, "tensor", [(p, p ^ 1) for p in range(parts)])

    def along(value, steps):
        first, last = (max(0, -steps), min(sections, sections - steps))
        return lax.ppermute(value, "section", [(s, s + steps) for s in range(first, last)])

    def place(step):
        return (rank ^ step) % BOX

    def gather_all(arrays, later):
        pieces = [{0: own} for own, heavy in arrays]
        heavies = [heavy for own, heavy in arrays]
        count = len(arrays)

        def step(index, target, source, pairs, link):
            if 0 <= index < count:
                hop(pieces[index][source], pairs, link, pieces[index], target)

        step(0, 1, 0, pair_all, PAIR_IN)
        step(0, 2, 0, inward, END_IN)
        step(0, 6, 0, across, ACROSS_IN)
        for index in range(count):
            step(index + 1, 1, 0, pair_all, PAIR_IN)
            step(index, 3, 1, inward, END_IN)
            step(index, 4, 2, across, ACROSS_IN)
            if heavies[index]:
                step(index, 7, 6, pair_inner, PAIR_IN)
            else:
                step(index, 7, 1, across, ACROSS_IN)
            step(index + 1, 2, 0, inward, END_IN)
            step(index + 1, 6, 0, across, ACROSS_IN)
            step(index, 5, 4, pair_inner, PAIR_IN)
        later, pieces[1][2] = lax.optimization_barrier((later, pieces[1][2]))
        wholes = []
        for found in pieces:
            own = found[0]
            shape = (own.shape[0], BOX, rows, own.shape[2])
            whole = jnp.broadcast_to(found[1][0, 0, 0], shape)
            for at, piece in found.items():
                whole = lax.dynamic_update_slice_in_dim(whole, piece[:, None], place(at), 1)
            whole = whole.reshape(shape[0], BOX * rows, shape[3])
            if boxes > 1:
                whole = lax.all_gather(
                    whole, "dp", axis=1, tiled=True, axis_index_groups=box_groups
                )
            wholes.append(whole)
        arrivals = [pieces[0][2], pieces[0][6], pieces[1][6], pieces[3][6]]
        return wholes, (later, arrivals)

    def starts_scatter(pair, pair_heavy):
        if boxes > 1:
            pair = lax.psum_scatter(
                pair, "dp", scatter_dimension=1, tiled=True, axis_index_groups=box_groups
            )

        apart_rows = pair.reshape(pair.shape[0], BOX, rows, pair.shape[2])

        def block(step, source=apart_rows):
            return lax.dynamic_index_in_dim(source, place(step), 1, False)

        def plus(step, name):
            source = tied(apart_rows, got, name)
            return low(wide(block(step, source)) + wide(got[name]))

        got = {}
        first = {step: block(step) for step in (3, 5, 7)}

        def gated_by_first(values):
            values, held = lax.optimization_barrier((values, first))
            first.update(held)
            return values

        def far_pair():
            hop(first[5], pair_inner, PAIR_LINK, got, FAR_PAIR)

        def near_pair():
            hop(first[7], pair_inner, PAIR_LINK, got, NEAR_PAIR)

        def far():
            hop(plus(4, FAR_PAIR), across, ACROSS_LINK, got, END)

        def near():
            near = plus(6, NEAR_PAIR) if pair_heavy else block(6)
            hop(near, across, ACROSS_LINK, got, MINE)

        def near_other():
            hop(first[7], across, ACROSS_LINK, got, THEIRS)

        def beside():
            own = block(1) if pair_heavy else plus(1, THEIRS)
            hop(own, pair_inner, PAIR_LINK, got, BESIDE)

        def end_pair():
            hop(first[3], outward, END_LINK, got, END_PAIR)

        def end_cross():
            hop(got[END_PAIR], pair_outer, None, got, CROSSED)

        def end_sum():
            hop(plus(2, END), outward, END_LINK, got, END_SUM)

        def result():
            inner_sum = wide(block(0)) + wide(got[MINE]) + wide(got[BESIDE])
            end_total = wide(got[END_SUM]) + wide(got[CROSSED])
            return jnp.where(is_inner, inner_sum, end_total)

        return SimpleNamespace(
            got=got,
            gate=gated_by_first,
            far_pair=far_pair,
            near_pair=near_pair,
            far=far,
            near=near,
            near_other=near_other,
            beside=beside,
            end_pair=end_pair,
            end_cross=end_cross,
            first=first,
            end_sum=end_sum,
            result=result,
        )

    def run(*steps):
        for step in steps:
            step()

    def two_core(pairs):
        return [(ranks + source, ranks + target) for source, target in pairs]

    def take_in(value):
        moved = lax.ppermute(value, ("tensor", "dp"), two_core(inward))
        return jnp.where(part == 0, value, moved)

    def hand_back(value, link=None, narrow=lambda leaf: leaf):
        moved = hop(narrow(value), two_core(outward), link, axis=("tensor", "dp")).astype(value.dtype)
        held = jnp.where(is_inner, value, moved)
        return jnp.where((part == 0) == is_inner, held, swap(held))

    own_rank = rank ^ (2 * part)
    other_rank = rank ^ (2 * (1 - part))
    (out_matrix, triple_matrix, up_matrix, down_matrix), held = gather_all(
        [
            (output_weight[0], True),
            (projection_weight[0].reshape(2, rows, 3 * local_width), False),
            (up_weight[0], True),
            (down_weight[0], False),
        ],
        tokens,
    )
    own_rank = rank ^ (2 * part)
    other_rank = rank ^ (2 * (1 - part))
    (out_matrix, triple_matrix, up_matrix, down_matrix), held = gather_all(
        [
            (output_weight[0], True),
            (projection_weight[0].reshape(2, rows, 3 * local_width), False),
            (up_weight[0], True),
            (down_weight[0], False),
        ],
        tokens,
    )
    tokens, arrivals = held
    both_all = spread_small(jnp.stack([times, text_counts]), 1, gates=arrivals[:2])
    both_all, arrivals[2] = lax.optimization_barrier((both_all, arrivals[2]))
    times_all, counts_all = both_all[0], both_all[1]
    sequences = take_in(tokens)
    top_grad = take_in(cotangent)

    onehot_all = (times_all[:, None] == jnp.arange(time_table.shape[0])[None, :]).astype(
        jnp.bfloat16
    )
    cond_all = jnp.dot(onehot_all, time_table, preferred_element_type=jnp.float32)
    cond_rows = lax.dynamic_slice_in_dim(cond_all, rank * rows, rows, 1)
    scaled_rows = jax.nn.silu(cond_rows).astype(jnp.bfloat16)
    adapt_part = jnp.einsum(
        "nd,sdkc->nskc", scaled_rows, modulation_weight[0], preferred_element_type=jnp.float32
    )

    def of_rank(stacked, index):
        return lax.dynamic_slice_in_dim(stacked, index * micro, micro, 0)

    def joined(mine, theirs, axis):
        return jnp.where(
            part == 0,
            jnp.concatenate([mine, theirs], axis),
            jnp.concatenate([theirs, mine], axis),
        )

    def pair_of_rank(index):
        return jnp.stack([of_rank(adapt_part, index), of_rank(adapt_part, index ^ 2)])

    adapt_terms = [pair_of_rank(rank)]
    for bit in range(1, ranks):
        pairs = [(r, r ^ bit) for r in range(ranks) if r ^ bit in inner]
        adapt_terms.append(hop(pair_of_rank(rank ^ bit), pairs))
    adapt_terms, arrivals[3] = lax.optimization_barrier((adapt_terms, arrivals[3]))
    adapt_pair = sum(adapt_terms)
    adapt_mine = jnp.where(part == 0, adapt_pair[0], adapt_pair[1])
    adapt_other = swap(jnp.where(part == 0, adapt_pair[1], adapt_pair[0]))
    adapt = joined(adapt_mine, adapt_other, 3)
    counts = jnp.concatenate([of_rank(counts_all, own_rank), of_rank(counts_all, other_rank)])
    group = parts * micro
    text_rows = -(-(length - IMG) // 16) * 16
    heads = local_width // HEAD

    def both(own):
        return [own, swap(own)]

    def own_total(partial):
        return wide(partial[0]) + wide(swap(partial[1]))

    def halves(like):
        return [leaf.shape[0] for leaf in like]

    def split(leaf):
        text = jnp.pad(leaf[:, IMG:], ((0, 0), (0, text_rows - (length - IMG)), (0, 0)))
        return [flat(leaf[:, :IMG]), flat(text)]

    def merge(sides):
        image, text = (leaf.reshape(micro, -1, width) for leaf in sides)
        return jnp.concatenate([image, text[:, : length - IMG]], 1)

    def by_sequence(leaf):
        return jnp.sum(leaf.reshape(micro, -1, leaf.shape[-1]), axis=1)

    def vector_of(side, index):
        return adapt[:, side, index][:, None]

    def apart(leaf):
        return leaf.reshape(micro, -1, leaf.shape[-1])

    def modulated(values, side, first):
        values = apart(values)
        result = norm_rows(values) * (1.0 + vector_of(side, first + 1))
        return flat(low(result + vector_of(side, first)))

    def gated(values, side, index):
        return flat(apart(values) * vector_of(side, index))

    def norm_back(values, grad, side, first):
        values, grad = (apart(values), apart(grad))
        centre = jnp.mean(values, axis=-1, keepdims=True)
        spread = values - centre
        variance = jnp.mean(spread * spread, axis=-1, keepdims=True)
        inverse = lax.rsqrt(variance + 1e-06)
        unit = spread * inverse
        inner_grad = grad * (1.0 + vector_of(side, first + 1))
        tilt = jnp.mean(inner_grad * unit, axis=-1, keepdims=True)
        level = jnp.mean(inner_grad, axis=-1, keepdims=True)
        result = inverse * (inner_grad - level - unit * tilt)
        return flat(result), jnp.sum(grad * unit, axis=1), jnp.sum(grad, axis=1)

    def layer_forward(sides):
        normed = [both(modulated(wide(sides[side]), side, 0)) for side in range(2)]
        packed = [
            product(
                normed[side], triple_matrix, side, False, 768, [[sum(halves(normed[side]))]], False
            )[0]
            for side in range(2)
        ]
        mixes = attention(counts, packed, heads)
        kept = SimpleNamespace(sides=sides, normed=normed, packed=packed, mixes=mixes)
        kept.branch, kept.middles, kept.seconds, kept.befores, kept.afters = ([], [], [], [], [])
        for side in range(2):
            branch = own_total(
                product([mixes[side]], out_matrix, side, True, 512, [halves(normed[side])], False)
            )
            middle = wide(sides[side]) + gated(branch, side, 2)
            kept.branch.append(branch)
            kept.middles.append(middle)
            kept.seconds.append(both(modulated(middle, side, 3)))
        for side in range(2):
            second = kept.seconds[side]
            rows_all = [sum(halves(second))]
            before, after = product(
                second, up_matrix, side, False, 512, [rows_all, rows_all], False, with_gelu
            )
            kept.befores.append(before)
            kept.afters.append(after)
        return kept

    def layer_feed(kept, gate):
        afters, gate = lax.optimization_barrier((kept.afters, gate))
        results = [None, None]
        feeds = [None, None]
        for side in (1, 0):
            partial = product(
                [afters[side]], down_matrix, side, True, 512, [halves(kept.seconds[side])], False
            )
            feeds[side] = own_total(partial)
            if side == 1:
                feeds[1], afters[0] = lax.optimization_barrier((feeds[1], afters[0]))
            results[side] = low(kept.middles[side] + gated(feeds[side], side, 5))
        return results, feeds

    def layer_backward(incoming, kept, feeds):
        final = feeds is not None
        up_grads, middle_grads, branch_grads, mix_grads = ([], [], [], [])
        vectors = [[None] * 6, [None] * 6]
        feed_grads = [both(low(gated(wide(incoming[side]), side, 5))) for side in range(2)]
        scatters = SimpleNamespace()
        if final:
            down = starts_scatter(turned_product(feed_grads, kept.afters, 512, True), False)
            feed_grads = down.gate(feed_grads)
            run(down.far_pair, down.near_other, down.near, down.end_pair)
            feed_grads[1] = tied(feed_grads[1], down.got, THEIRS)
            scatters.down = down
        for side in range(2):
            feed_grad = feed_grads[side]
            rows_all = [[sum(halves(feed_grad))]]
            up_grad = product(
                feed_grad,
                down_matrix,
                side,
                False,
                512,
                rows_all,
                final,
                times_slope,
                [kept.befores[side]],
            )[0]
            up_grads.append(up_grad)
        if final:
            up_gradient = turned_product(kept.seconds, up_grads, 512, True)
        second_parts = [
            product([up_grads[side]], up_matrix, side, True, 512, [halves(feed_grads[side])], final)
            for side in range(2)
        ]
        if final:
            up = starts_scatter(up_gradient, True)
            scatters.up = up
            run(up.far_pair, up.near_pair, up.end_pair)
            run(down.far)
            run(up.far)
            run(down.beside)
            run(up.near)
        for side in range(2):
            upstream = wide(incoming[side])
            feed_grad = feed_grads[side]
            up_grad = up_grads[side]
            rows_all = [[sum(halves(feed_grad))]]
            if final:
                vectors[side][5] = by_sequence(upstream * feeds[side])
            else:
                vectors[side][5] = jnp.zeros((micro, width), jnp.float32)
            second_grad = own_total(second_parts[side])
            middle_part, vectors[side][4], vectors[side][3] = norm_back(
                kept.middles[side], second_grad, side, 3
            )
            middle_grad = upstream + middle_part
            branch_grad = both(low(gated(middle_grad, side, 2)))
            middle_grads.append(middle_grad)
            branch_grads.append(branch_grad)
            vectors[side][2] = by_sequence(middle_grad * kept.branch[side])
            mix_grads.append(
                product(branch_grad, out_matrix, side, False, 256, rows_all, final)[0]
            )
        if final:
            mix_grads[0] = tied(mix_grads[0], down.got, MINE)
        triples = list(attention_back(counts, kept.packed, mix_grads, heads, final))
        if final:
            run(down.end_sum)
            run(up.end_sum)
        results = []
        partials = []
        for side in range(2):
            partials.append(
                product(
                    [triples[side]],
                    triple_matrix,
                    side,
                    True,
                    512,
                    [halves(branch_grads[side])],
                    final,
                )
            )
        for side in range(2):
            first_grad = own_total(partials[side])
            input_part, vectors[side][1], vectors[side][0] = norm_back(
                wide(kept.sides[side]), first_grad, side, 0
            )
            results.append(middle_grads[side] + input_part)
        vectors = jnp.stack([jnp.stack(v, 1) for v in vectors], 1)
        return (results, vectors, triples, branch_grads, scatters)

    first_in = split(sequences)
    entering = first_in
    for phase in range(sections):
        if phase:
            received = [None, None]
            for side in (1, 0):
                received[side] = along(leaving[side], 1)
            entering = [
                jnp.where(section == 0, leaf, moved) for leaf, moved in zip(first_in, received)
            ]
        kept = layer_forward(entering)
        if phase + 1 < sections:
            leaving, feeds = layer_feed(kept, ())
    last_grad = split(top_grad)
    upstream = last_grad
    feeds = None
    sent = ()
    for phase in range(sections):
        if phase:
            sent = [low(leaf) for leaf in input_grads]
            received = [along(leaf, -1) for leaf in sent]
            upstream = [
                jnp.where(section == sections - 1, leaf, moved)
                for leaf, moved in zip(last_grad, received)
            ]
        if phase + 1 == sections:
            leaving, feeds = layer_feed(kept, sent)
        input_grads, vectors, triples, branch_grads, scatters = layer_backward(
            upstream, kept, feeds
        )
    activations = hand_back(merge(leaving))[None]

    down, up = scatters.down, scatters.up
    triple = starts_scatter(turned_product(kept.normed, triples, 768, True), False)
    out = starts_scatter(turned_product(branch_grads, kept.mixes, 256, True), True)
    vectors = low(vectors)
    halved = (vectors[..., :local_width], vectors[..., local_width:])
    mine = jnp.where(part == 0, halved[0], halved[1])
    theirs = swap(jnp.where(part == 0, halved[1], halved[0]))
    cores = jnp.where(part == 0, jnp.stack([mine, theirs]), jnp.stack([theirs, mine]))
    found = {0: cores}
    run(down.end_cross)
    run(up.beside, up.end_cross)
    hop(cores, pair_inner, PAIR_LINK, found, 1)
    triple.first[7] = tied(triple.first[7], up.got, BESIDE)
    triple.first[3] = tied(triple.first[3], down.got, CROSSED)
    run(triple.far_pair, triple.near_other, triple.end_pair, triple.end_cross)
    run(out.far_pair, out.near_pair)
    hop(found[0], across, ACROSS_LINK, found, 6)
    hop(found[1], across, ACROSS_LINK, found, 7)
    run(triple.far, triple.near, triple.beside)
    hop(jnp.stack([found[k] for k in (0, 1, 6, 7)]), outward, END_LINK, found, ENDED)
    out.first[3] = tied(out.first[3], up.got, CROSSED)
    run(out.end_pair, out.end_cross)
    input_gradient = hand_back(merge(input_grads), END_LINK, low)[None]
    run(triple.end_sum)
    out.got[FAR_PAIR] = tied(out.got[FAR_PAIR], triple.got, BESIDE)
    run(out.far, out.near, out.beside, out.end_sum)
    base = jnp.where(is_inner, rank, rank ^ 2)
    every = jnp.zeros((BOX,) + cores.shape, cores.dtype)
    for index, k in enumerate((0, 1, 6, 7)):
        entry = jnp.where(is_inner, found[k], found[ENDED][index])[None]
        every = lax.dynamic_update_slice_in_dim(every, entry, (base ^ k) % BOX, 0)
    if boxes > 1:
        every = lax.all_gather(every, "dp", axis=0, tiled=True, axis_index_groups=box_groups)
    adapt_every = jnp.concatenate(
        [every[r, 0] if r in inner else every[r ^ 2, 1] for r in range(ranks)], 0
    )
    modulation_gradient = jnp.einsum(
        "nr,nskc->srkc", scaled_rows, adapt_every, preferred_element_type=jnp.float32
    )[None]
    cond_rows_grad = jnp.einsum(
        "nskc,sdkc->nd", adapt_every, modulation_weight[0], preferred_element_type=jnp.float32
    )
    cond_rows_grad = tied(cond_rows_grad, out.got, MINE)
    cond_rows_grad = cond_rows_grad + swap(cond_rows_grad)
    section_grad = cond_rows_grad
    for steps in range(1, sections):
        turned = [(s, (s + steps) % sections) for s in range(sections)]
        section_grad = section_grad + lax.ppermute(cond_rows_grad, "section", turned)
    cond_grad = spread_small(silu_slope(cond_rows) * section_grad, 1)
    down_gradient = down.result()[None]
    up_gradient = up.result()[None]
    columns = width // (sections * parts * ranks)
    first_column = ((section * parts + part) * ranks + rank) * columns
    table_gradient = jnp.dot(
        wide(onehot_all).T,
        lax.dynamic_slice_in_dim(cond_grad, first_column, columns, 1),
        precision=lax.Precision.HIGHEST,
    )
    output_gradient = out.result()[None]
    projection_gradient = triple.result().reshape(2, rows, 3, local_width)[None]
    return (
        activations,
        input_gradient,
        table_gradient,
        modulation_gradient,
        projection_gradient,
        output_gradient,
        up_gradient,
        down_gradient,
    )


def solution(mesh):
    in_specs = (
        P("dp", None, None),
        P("dp", None, None),
        P("dp"),
        P("dp"),
        P(),
        P("section", None, "dp", None, "tensor"),
        P("section", None, "dp", None, "tensor"),
        P("section", None, "dp", "tensor"),
        P("section", None, "dp", "tensor"),
        P("section", None, "dp", "tensor"),
    )
    out_specs = (
        P("section", "dp", None, None),
        P("section", "dp", None, None),
        P(None, ("section", "tensor", "dp")),
        P("section", None, "dp", None, "tensor"),
        P("section", None, "dp", None, "tensor"),
        P("section", None, "dp", "tensor"),
        P("section", None, "dp", "tensor"),
        P("section", None, "dp", "tensor"),
    )
    return jax.shard_map(
        on_device, mesh=mesh, in_specs=in_specs, out_specs=out_specs, check_vma=False
    )
```

```python
import functools
from types import SimpleNamespace

import jax
import jax.numpy as jnp
from jax import lax
from jax.experimental import pallas as pl
from jax.experimental.pallas import tpu as pltpu
from jax.sharding import PartitionSpec as P

HEAD = 64
IMG = 128
BOX = 8
(FAR_PAIR, NEAR_PAIR, END, MINE, THEIRS, BESIDE, END_SUM, END_PAIR, CROSSED) = range(100, 109)
(PAIR_IN, END_IN, ACROSS_IN, PAIR_LINK, END_LINK, ACROSS_LINK, ENDED) = range(109, 116)
VMEM_LIMIT = 40 * 1024 * 1024


def norm_rows(values):
    centre = jnp.mean(values, axis=-1, keepdims=True)
    spread = values - centre
    variance = jnp.mean(spread * spread, axis=-1, keepdims=True)
    return spread * lax.rsqrt(variance + 1e-06)


def gelu_tanh(values):
    inner = 0.7978845608028654 * (values + 0.044715 * values * values * values)
    return 0.5 * values * (1.0 + jnp.tanh(inner))


def gelu_slope(values):
    square = values * values
    bend = jnp.tanh(0.7978845608028654 * (values + 0.044715 * values * square))
    return 0.5 * (1.0 + bend) + 0.5 * values * (1.0 - bend * bend) * (
        0.7978845608028654 * (1.0 + 0.134145 * square)
    )


def silu_slope(values):
    sigma = jax.nn.sigmoid(values)
    return sigma * (1.0 + values * (1.0 - sigma))


def left_dot(left, weight):
    return lax.dot_general(
        left, weight, (((1,), (0,)), ((), ())), preferred_element_type=jnp.float32
    )


def right_dot(left, weight):
    return lax.dot_general(
        left, weight, (((1,), (1,)), ((), ())), preferred_element_type=jnp.float32
    )


def rows_dot(left, right):
    return lax.dot_general(
        left, right, (((0,), (0,)), ((), ())), preferred_element_type=jnp.float32
    )


def flat(leaf):
    return leaf.reshape(-1, leaf.shape[-1])


def low(leaf):
    return leaf.astype(jnp.bfloat16)


def wide(leaf):
    return leaf.astype(jnp.float32)


def pair_mask(rows, half):
    lanes = lax.broadcasted_iota(jnp.int32, (rows, 2 * HEAD), 1)
    return lanes < HEAD if half == 0 else lanes >= HEAD


def only_half(leaf, half):
    return jnp.where(pair_mask(leaf.shape[0], half), leaf, jnp.zeros_like(leaf))


def stacked_rows(refs, column):
    lanes = pl.ds(column, 2 * HEAD)
    return jnp.concatenate([ref[:, lanes] for ref in refs], 0)


def put_rows(refs, column, value):
    start = 0
    for ref in refs:
        stop = start + ref.shape[0]
        ref[:, pl.ds(column, 2 * HEAD)] = value[start:stop]
        start = stop


def attention_kernel(counts, image, text, mixed_image, mixed_text):
    width = mixed_image.shape[1]
    total = image.shape[0] + text.shape[0]
    bound = IMG + counts[pl.program_id(0)]
    live = lax.broadcasted_iota(jnp.int32, (2 * total, total), 1) < bound
    for column in range(0, width, 2 * HEAD):
        queries = stacked_rows((image, text), column) * HEAD ** (-0.5)
        keys = stacked_rows((image, text), width + column)
        values = stacked_rows((image, text), 2 * width + column)
        asked = jnp.concatenate([only_half(queries, half) for half in range(2)], 0)
        scores = jnp.where(live, right_dot(asked, keys), -1e30)
        weights = jnp.exp(scores - jnp.max(scores, axis=-1, keepdims=True))
        share = 1.0 / jnp.sum(weights, axis=-1, keepdims=True)
        mixed = left_dot(low(weights), values) * share
        mixed = low(jnp.where(pair_mask(total, 0), mixed[:total], mixed[total:]))
        put_rows((mixed_image, mixed_text), column, mixed)


def attention_back_kernel(
    counts, image, text, grad_image, grad_text, out_image, out_text
):
    width = grad_image.shape[1]
    total = image.shape[0] + text.shape[0]
    bound = IMG + counts[pl.program_id(0)]
    live = lax.broadcasted_iota(jnp.int32, (total, 2 * total), 0) < bound
    scale = HEAD ** (-0.5)
    for column in range(0, width, 2 * HEAD):
        queries = stacked_rows((image, text), column) * scale
        keys = stacked_rows((image, text), width + column)
        values = stacked_rows((image, text), 2 * width + column)
        grads = stacked_rows((grad_image, grad_text), column)
        asked = jnp.concatenate([only_half(queries, half) for half in range(2)], 0)
        given = jnp.concatenate([only_half(grads, half) for half in range(2)], 0)
        scores = jnp.where(live, right_dot(keys, asked), -1e30)
        soft = jnp.exp(scores - jnp.max(scores, axis=0, keepdims=True))
        soft = soft * (1.0 / jnp.sum(soft, axis=0, keepdims=True))
        prob_grad = right_dot(values, given)
        drop = jnp.sum(prob_grad * soft, axis=0, keepdims=True)
        score_grad = low(soft * (prob_grad - drop))
        query_grad = rows_dot(score_grad, keys) * scale
        query_grad = jnp.where(pair_mask(total, 0), query_grad[:total], query_grad[total:])
        refs = (out_image, out_text)
        put_rows(refs, column, low(query_grad))
        put_rows(refs, width + column, low(left_dot(score_grad, asked)))
        put_rows(refs, 2 * width + column, low(left_dot(low(soft), given)))


def by_sequence_call(kernel, counts, inputs, widths, name, matmuls, light):
    group = counts.shape[0]

    def spec(rows, width):
        return pl.BlockSpec((rows, width), lambda n, counts: (n, 0))

    rows = [leaf.shape[0] // group for leaf in inputs[:2]]
    total = sum(rows)
    return pl.pallas_call(
        kernel,
        grid_spec=pltpu.PrefetchScalarGridSpec(
            num_scalar_prefetch=1,
            grid=(group,),
            in_specs=[spec(leaf.shape[0] // group, leaf.shape[1]) for leaf in inputs],
            out_specs=[spec(count, widths) for count in rows],
        ),
        out_shape=[
            jax.ShapeDtypeStruct((group * count, widths), jnp.bfloat16) for count in rows
        ],
        compiler_params=pltpu.CompilerParams(vmem_limit_bytes=48 * 1024 * 1024),
        cost_estimate=estimate(
            7 * matmuls * group * total * total * 12 * 2 * HEAD,
            sum(leaf.size for leaf in inputs) + group * total * widths,
            light,
        ),
        name=name,
    )(counts, *inputs)


def attention(counts, packed, heads):
    return by_sequence_call(
        attention_kernel, counts, list(packed), heads * HEAD, "attention", 2, False
    )


def attention_back(counts, packed, grads, heads, light):
    return by_sequence_call(
        attention_back_kernel,
        counts,
        list(packed) + list(grads),
        3 * heads * HEAD,
        "attention_back",
        5,
        light,
    )


def joined_rows(refs):
    values = [ref[...] for ref in refs]
    return values[0] if len(values) == 1 else jnp.concatenate(values, 0)


def store_rows(refs, value):
    start = 0
    for ref in refs:
        stop = start + ref.shape[0]
        ref[...] = value[start:stop].astype(ref.dtype)
        start = stop


def product_kernel(counts, dims, finish, *refs):
    lefts, extras, outs = counts
    right = refs[lefts][...]
    total = lax.dot_general(
        joined_rows(refs[:lefts]), right, (dims, ((), ())), preferred_element_type=jnp.float32
    )
    refs = refs[lefts + 1 :]
    results = finish(total, *[ref[...] for ref in refs[:extras]])
    refs = refs[extras:]
    for count, value in zip(outs, results):
        store_rows(refs[:count], value)
        refs = refs[count:]


def turned_kernel(lefts, tiles, *refs):
    turned = refs[-len(lefts) :]
    result = refs[-len(lefts) - 1]
    step = pl.program_id(0)
    start = 0
    for side, count in enumerate(lefts):
        sources = refs[start : start + count]
        right = refs[start + count]
        start += count + 1

        @pl.when(step == side * tiles)
        def _(sources=sources, held=turned[side]):
            held[...] = joined_rows(sources).T

        @pl.when(jnp.logical_and(step >= side * tiles, step < (side + 1) * tiles))
        def _(right=right, held=turned[side]):
            result[...] = low(left_dot(held[...], right[...]))


def estimate(flops, values, light):
    return pl.CostEstimate(flops=2 * flops, bytes_accessed=2 * values, transcendentals=0)


def product(lefts, right, side, turned, tile, outs, light, finish=None, extras=()):
    depth = lefts[0].shape[1]
    width = right.shape[1] if turned else right.shape[2]
    if turned:
        right_spec = pl.BlockSpec((None, tile, depth), lambda n: (side, n, 0))
    else:
        right_spec = pl.BlockSpec((None, depth, tile), lambda n: (side, 0, n))
    rows = sum(leaf.shape[0] for leaf in lefts)
    counts = [count for group in outs for count in group]
    kernel = functools.partial(
        product_kernel,
        (len(lefts), len(extras), [len(group) for group in outs]),
        ((1,), (1 if turned else 0,)),
        finish or (lambda total: (total,)),
    )
    return pl.pallas_call(
        kernel,
        grid=(width // tile,),
        in_specs=[pl.BlockSpec(leaf.shape, lambda n: (0, 0)) for leaf in lefts]
        + [right_spec]
        + [pl.BlockSpec((rows, tile), lambda n: (0, n)) for leaf in extras],
        out_specs=[pl.BlockSpec((count, tile), lambda n: (0, n)) for count in counts],
        out_shape=[jax.ShapeDtypeStruct((count, width), jnp.bfloat16) for count in counts],
        compiler_params=pltpu.CompilerParams(vmem_limit_bytes=VMEM_LIMIT),
        cost_estimate=estimate(2 * rows * depth * width, depth * width + 2 * rows * width, light),
    )(*lefts, right, *extras)


def turned_product(lefts, rights, tile, light):
    depth, width = lefts[0][0].shape[1], rights[0].shape[1]
    tiles = width // tile
    in_specs, operands, scratch = ([], [], [])
    for side, (left, right) in enumerate(zip(lefts, rights)):
        first = side * tiles
        in_specs += [pl.BlockSpec(leaf.shape, lambda n: (0, 0)) for leaf in left]
        in_specs.append(
            pl.BlockSpec(
                (right.shape[0], tile), lambda n, first=first: (0, jnp.clip(n - first, 0, tiles - 1))
            )
        )
        operands += list(left) + [right]
        scratch.append(pltpu.VMEM((depth, right.shape[0]), jnp.bfloat16))
    rows = sum(right.shape[0] for right in rights)
    return pl.pallas_call(
        functools.partial(turned_kernel, [len(left) for left in lefts], tiles),
        grid=(len(lefts) * tiles,),
        in_specs=in_specs,
        out_specs=pl.BlockSpec((None, depth, tile), lambda n: (n // tiles, 0, n % tiles)),
        out_shape=jax.ShapeDtypeStruct((len(lefts), depth, width), jnp.bfloat16),
        scratch_shapes=scratch,
        compiler_params=pltpu.CompilerParams(vmem_limit_bytes=VMEM_LIMIT),
        cost_estimate=estimate(2 * rows * depth * width, depth * width, light),
    )(*operands)


def with_gelu(before):
    return before, gelu_tanh(before)


def times_slope(after_grad, before):
    return (after_grad * gelu_slope(wide(before)),)


def on_device(
    tokens,
    cotangent,
    times,
    text_counts,
    time_table,
    modulation_weight,
    projection_weight,
    output_weight,
    up_weight,
    down_weight,
):
    micro, length, width = tokens.shape
    sections = lax.axis_size("section")
    section = lax.axis_index("section")
    parts = lax.axis_size("tensor")
    part = lax.axis_index("tensor")
    ranks = lax.axis_size("dp")
    rank = lax.axis_index("dp")
    local_width = projection_weight.shape[4]
    rows = projection_weight.shape[2]

    inner = [r for r in range(ranks) if (r >> 1) % 4 in (1, 2)]
    outer = [r for r in range(ranks) if (r >> 1) % 4 in (0, 3)]
    is_inner = jnp.logical_or((rank >> 1) % 4 == 1, (rank >> 1) % 4 == 2)
    pair_all = [(r, r ^ 1) for r in range(ranks)]
    pair_inner = [(r, r ^ 1) for r in inner]
    pair_outer = [(r, r ^ 1) for r in outer]
    inward = [(r, r ^ 2) for r in outer]
    outward = [(r, r ^ 2) for r in inner]
    across = [(r, r ^ 6) for r in inner]
    boxes = ranks // BOX
    box_groups = [[b * BOX + i for b in range(boxes)] for i in range(BOX)]

    links = {}
    depths = {}

    def tied(value, holder, name):
        value, holder[name] = lax.optimization_barrier((value, holder[name]))
        return value

    def hop(value, pairs, link=None, holder=None, name=0, axis="dp"):
        queue = links.setdefault(link, [])
        depth = depths.get(link, 1)
        if link is not None and len(queue) >= depth:
            value = tied(value, *queue[-depth])
        moved = lax.ppermute(value, axis, pairs)
        holder = {} if holder is None else holder
        holder[name] = moved
        if link is not None:
            queue.append((holder, name))
        return moved

    def by_bits(bit):
        return [(r, r ^ bit) for r in range(ranks)]

    def spread_small(value, axis, queued=False, gates=()):
        bit = 1
        gates = list(gates)
        while bit < ranks:
            link = {1: PAIR_LINK, 2: END_LINK, 4: ACROSS_LINK}.get(bit) if queued else None
            if bit > 1 and gates:
                value, _ = lax.optimization_barrier((value, gates.pop(0)))
            other = hop(value, by_bits(bit), link)
            value = jnp.where(
                (rank & bit) == 0,
                jnp.concatenate([value, other], axis),
                jnp.concatenate([other, value], axis),
            )
            bit *= 2
        return value

    def swap(value):
        return lax.ppermute(value, "tensor", [(p, p ^ 1) for p in range(parts)])

    def along(value, steps):
        first, last = (max(0, -steps), min(sections, sections - steps))
        return lax.ppermute(value, "section", [(s, s + steps) for s in range(first, last)])

    def place(step):
        return (rank ^ step) % BOX

    def gather_all(arrays, later):
        pieces = [{0: own} for own, heavy in arrays]
        heavies = [heavy for own, heavy in arrays]
        count = len(arrays)

        def step(index, target, source, pairs, link):
            if 0 <= index < count:
                hop(pieces[index][source], pairs, link, pieces[index], target)

        step(0, 1, 0, pair_all, PAIR_IN)
        step(0, 2, 0, inward, END_IN)
        step(0, 6, 0, across, ACROSS_IN)
        for index in range(count):
            step(index + 1, 1, 0, pair_all, PAIR_IN)
            step(index, 3, 1, inward, END_IN)
            step(index, 4, 2, across, ACROSS_IN)
            if heavies[index]:
                step(index, 7, 6, pair_inner, PAIR_IN)
            else:
                step(index, 7, 1, across, ACROSS_IN)
            step(index + 1, 2, 0, inward, END_IN)
            step(index + 1, 6, 0, across, ACROSS_IN)
            step(index, 5, 4, pair_inner, PAIR_IN)
        later, pieces[1][2] = lax.optimization_barrier((later, pieces[1][2]))
        wholes = []
        for found in pieces:
            own = found[0]
            shape = (own.shape[0], BOX, rows, own.shape[2])
            whole = jnp.broadcast_to(found[1][0, 0, 0], shape)
            for at, piece in found.items():
                whole = lax.dynamic_update_slice_in_dim(whole, piece[:, None], place(at), 1)
            whole = whole.reshape(shape[0], BOX * rows, shape[3])
            if boxes > 1:
                whole = lax.all_gather(
                    whole, "dp", axis=1, tiled=True, axis_index_groups=box_groups
                )
            wholes.append(whole)
        arrivals = [pieces[0][2], pieces[0][6], pieces[1][6], pieces[3][6]]
        return wholes, (later, arrivals)

    def starts_scatter(pair, pair_heavy):
        if boxes > 1:
            pair = lax.psum_scatter(
                pair, "dp", scatter_dimension=1, tiled=True, axis_index_groups=box_groups
            )

        apart_rows = pair.reshape(pair.shape[0], BOX, rows, pair.shape[2])

        def block(step, source=apart_rows):
            return lax.dynamic_index_in_dim(source, place(step), 1, False)

        def plus(step, name):
            source = tied(apart_rows, got, name)
            return low(wide(block(step, source)) + wide(got[name]))

        got = {}
        first = {step: block(step) for step in (3, 5, 7)}

        def gated_by_first(values):
            values, held = lax.optimization_barrier((values, first))
            first.update(held)
            return values

        def far_pair():
            hop(first[5], pair_inner, PAIR_LINK, got, FAR_PAIR)

        def near_pair():
            hop(first[7], pair_inner, PAIR_LINK, got, NEAR_PAIR)

        def far():
            hop(plus(4, FAR_PAIR), across, ACROSS_LINK, got, END)

        def near():
            near = plus(6, NEAR_PAIR) if pair_heavy else block(6)
            hop(near, across, ACROSS_LINK, got, MINE)

        def near_other():
            hop(first[7], across, ACROSS_LINK, got, THEIRS)

        def beside():
            own = block(1) if pair_heavy else plus(1, THEIRS)
            hop(own, pair_inner, PAIR_LINK, got, BESIDE)

        def end_pair():
            hop(first[3], outward, END_LINK, got, END_PAIR)

        def end_cross():
            hop(got[END_PAIR], pair_outer, None, got, CROSSED)

        def end_sum():
            hop(plus(2, END), outward, END_LINK, got, END_SUM)

        def result():
            inner_sum = wide(block(0)) + wide(got[MINE]) + wide(got[BESIDE])
            end_total = wide(got[END_SUM]) + wide(got[CROSSED])
            return jnp.where(is_inner, inner_sum, end_total)

        return SimpleNamespace(
            got=got,
            gate=gated_by_first,
            far_pair=far_pair,
            near_pair=near_pair,
            far=far,
            near=near,
            near_other=near_other,
            beside=beside,
            end_pair=end_pair,
            end_cross=end_cross,
            first=first,
            end_sum=end_sum,
            result=result,
        )

    def run(*steps):
        for step in steps:
            step()

    def two_core(pairs):
        return [(ranks + source, ranks + target) for source, target in pairs]

    def take_in(value):
        moved = lax.ppermute(value, ("tensor", "dp"), two_core(inward))
        return jnp.where(part == 0, value, moved)

    def hand_back(value, link=None, narrow=lambda leaf: leaf):
        moved = hop(narrow(value), two_core(outward), link, axis=("tensor", "dp")).astype(value.dtype)
        held = jnp.where(is_inner, value, moved)
        return jnp.where((part == 0) == is_inner, held, swap(held))

    own_rank = rank ^ (2 * part)
    other_rank = rank ^ (2 * (1 - part))
    (out_matrix, triple_matrix, up_matrix, down_matrix), held = gather_all(
        [
            (output_weight[0], True),
            (projection_weight[0].reshape(2, rows, 3 * local_width), False),
            (up_weight[0], True),
            (down_weight[0], False),
        ],
        tokens,
    )
    own_rank = rank ^ (2 * part)
    other_rank = rank ^ (2 * (1 - part))
    (out_matrix, triple_matrix, up_matrix, down_matrix), held = gather_all(
        [
            (output_weight[0], True),
            (projection_weight[0].reshape(2, rows, 3 * local_width), False),
            (up_weight[0], True),
            (down_weight[0], False),
        ],
        tokens,
    )
    tokens, arrivals = held
    both_all = spread_small(jnp.stack([times, text_counts]), 1, gates=arrivals[:2])
    both_all, arrivals[2] = lax.optimization_barrier((both_all, arrivals[2]))
    times_all, counts_all = both_all[0], both_all[1]
    sequences = take_in(tokens)
    top_grad = take_in(cotangent)

    onehot_all = (times_all[:, None] == jnp.arange(time_table.shape[0])[None, :]).astype(
        jnp.bfloat16
    )
    cond_all = jnp.dot(onehot_all, time_table, preferred_element_type=jnp.float32)
    cond_rows = lax.dynamic_slice_in_dim(cond_all, rank * rows, rows, 1)
    scaled_rows = jax.nn.silu(cond_rows).astype(jnp.bfloat16)
    adapt_part = jnp.einsum(
        "nd,sdkc->nskc", scaled_rows, modulation_weight[0], preferred_element_type=jnp.float32
    )

    def of_rank(stacked, index):
        return lax.dynamic_slice_in_dim(stacked, index * micro, micro, 0)

    def joined(mine, theirs, axis):
        return jnp.where(
            part == 0,
            jnp.concatenate([mine, theirs], axis),
            jnp.concatenate([theirs, mine], axis),
        )

    def pair_of_rank(index):
        return jnp.stack([of_rank(adapt_part, index), of_rank(adapt_part, index ^ 2)])

    adapt_terms = [pair_of_rank(rank)]
    for bit in range(1, ranks):
        pairs = [(r, r ^ bit) for r in range(ranks) if r ^ bit in inner]
        adapt_terms.append(hop(pair_of_rank(rank ^ bit), pairs))
    adapt_terms, arrivals[3] = lax.optimization_barrier((adapt_terms, arrivals[3]))
    adapt_pair = sum(adapt_terms)
    adapt_mine = jnp.where(part == 0, adapt_pair[0], adapt_pair[1])
    adapt_other = swap(jnp.where(part == 0, adapt_pair[1], adapt_pair[0]))
    adapt = joined(adapt_mine, adapt_other, 3)
    counts = jnp.concatenate([of_rank(counts_all, own_rank), of_rank(counts_all, other_rank)])
    group = parts * micro
    text_rows = -(-(length - IMG) // 16) * 16
    heads = local_width // HEAD

    def both(own):
        return [own, swap(own)]

    def own_total(partial):
        return wide(partial[0]) + wide(swap(partial[1]))

    def halves(like):
        return [leaf.shape[0] for leaf in like]

    def split(leaf):
        text = jnp.pad(leaf[:, IMG:], ((0, 0), (0, text_rows - (length - IMG)), (0, 0)))
        return [flat(leaf[:, :IMG]), flat(text)]

    def merge(sides):
        image, text = (leaf.reshape(micro, -1, width) for leaf in sides)
        return jnp.concatenate([image, text[:, : length - IMG]], 1)

    def by_sequence(leaf):
        return jnp.sum(leaf.reshape(micro, -1, leaf.shape[-1]), axis=1)

    def vector_of(side, index):
        return adapt[:, side, index][:, None]

    def apart(leaf):
        return leaf.reshape(micro, -1, leaf.shape[-1])

    def modulated(values, side, first):
        values = apart(values)
        result = norm_rows(values) * (1.0 + vector_of(side, first + 1))
        return flat(low(result + vector_of(side, first)))

    def gated(values, side, index):
        return flat(apart(values) * vector_of(side, index))

    def norm_back(values, grad, side, first):
        values, grad = (apart(values), apart(grad))
        centre = jnp.mean(values, axis=-1, keepdims=True)
        spread = values - centre
        variance = jnp.mean(spread * spread, axis=-1, keepdims=True)
        inverse = lax.rsqrt(variance + 1e-06)
        unit = spread * inverse
        inner_grad = grad * (1.0 + vector_of(side, first + 1))
        tilt = jnp.mean(inner_grad * unit, axis=-1, keepdims=True)
        level = jnp.mean(inner_grad, axis=-1, keepdims=True)
        result = inverse * (inner_grad - level - unit * tilt)
        return flat(result), jnp.sum(grad * unit, axis=1), jnp.sum(grad, axis=1)

    def layer_forward(sides):
        normed = [both(modulated(wide(sides[side]), side, 0)) for side in range(2)]
        packed = [
            product(
                normed[side], triple_matrix, side, False, 768, [[sum(halves(normed[side]))]], False
            )[0]
            for side in range(2)
        ]
        mixes = attention(counts, packed, heads)
        kept = SimpleNamespace(sides=sides, normed=normed, packed=packed, mixes=mixes)
        kept.branch, kept.middles, kept.seconds, kept.befores, kept.afters = ([], [], [], [], [])
        for side in range(2):
            branch = own_total(
                product([mixes[side]], out_matrix, side, True, 512, [halves(normed[side])], False)
            )
            middle = wide(sides[side]) + gated(branch, side, 2)
            kept.branch.append(branch)
            kept.middles.append(middle)
            kept.seconds.append(both(modulated(middle, side, 3)))
        for side in range(2):
            second = kept.seconds[side]
            rows_all = [sum(halves(second))]
            before, after = product(
                second, up_matrix, side, False, 512, [rows_all, rows_all], False, with_gelu
            )
            kept.befores.append(before)
            kept.afters.append(after)
        return kept

    def layer_feed(kept, gate):
        afters, gate = lax.optimization_barrier((kept.afters, gate))
        results = [None, None]
        feeds = [None, None]
        for side in (1, 0):
            partial = product(
                [afters[side]], down_matrix, side, True, 512, [halves(kept.seconds[side])], False
            )
            feeds[side] = own_total(partial)
            if side == 1:
                feeds[1], afters[0] = lax.optimization_barrier((feeds[1], afters[0]))
            results[side] = low(kept.middles[side] + gated(feeds[side], side, 5))
        return results, feeds

    def layer_backward(incoming, kept, feeds):
        final = feeds is not None
        up_grads, middle_grads, branch_grads, mix_grads = ([], [], [], [])
        vectors = [[None] * 6, [None] * 6]
        feed_grads = [both(low(gated(wide(incoming[side]), side, 5))) for side in range(2)]
        scatters = SimpleNamespace()
        if final:
            down = starts_scatter(turned_product(feed_grads, kept.afters, 512, True), False)
            feed_grads = down.gate(feed_grads)
            run(down.far_pair, down.near_other, down.near, down.end_pair)
            feed_grads[1] = tied(feed_grads[1], down.got, THEIRS)
            scatters.down = down
        for side in range(2):
            feed_grad = feed_grads[side]
            rows_all = [[sum(halves(feed_grad))]]
            up_grad = product(
                feed_grad,
                down_matrix,
                side,
                False,
                512,
                rows_all,
                final,
                times_slope,
                [kept.befores[side]],
            )[0]
            up_grads.append(up_grad)
        if final:
            up_gradient = turned_product(kept.seconds, up_grads, 512, True)
        second_parts = [
            product([up_grads[side]], up_matrix, side, True, 512, [halves(feed_grads[side])], final)
            for side in range(2)
        ]
        if final:
            up = starts_scatter(up_gradient, True)
            scatters.up = up
            run(up.far_pair, up.near_pair, up.end_pair)
            run(down.far)
            run(up.far)
            run(down.beside)
            run(up.near)
        for side in range(2):
            upstream = wide(incoming[side])
            feed_grad = feed_grads[side]
            up_grad = up_grads[side]
            rows_all = [[sum(halves(feed_grad))]]
            if final:
                vectors[side][5] = by_sequence(upstream * feeds[side])
            else:
                vectors[side][5] = jnp.zeros((micro, width), jnp.float32)
            second_grad = own_total(second_parts[side])
            middle_part, vectors[side][4], vectors[side][3] = norm_back(
                kept.middles[side], second_grad, side, 3
            )
            middle_grad = upstream + middle_part
            branch_grad = both(low(gated(middle_grad, side, 2)))
            middle_grads.append(middle_grad)
            branch_grads.append(branch_grad)
            vectors[side][2] = by_sequence(middle_grad * kept.branch[side])
            mix_grads.append(
                product(branch_grad, out_matrix, side, False, 256, rows_all, final)[0]
            )
        triples = list(attention_back(counts, kept.packed, mix_grads, heads, final))
        if final:
            run(down.end_sum)
            run(up.end_sum)
        results = []
        partials = []
        for side in range(2):
            partials.append(
                product(
                    [triples[side]],
                    triple_matrix,
                    side,
                    True,
                    512,
                    [halves(branch_grads[side])],
                    final,
                )
            )
        for side in range(2):
            first_grad = own_total(partials[side])
            input_part, vectors[side][1], vectors[side][0] = norm_back(
                wide(kept.sides[side]), first_grad, side, 0
            )
            results.append(middle_grads[side] + input_part)
        vectors = jnp.stack([jnp.stack(v, 1) for v in vectors], 1)
        return (results, vectors, triples, branch_grads, scatters)

    first_in = split(sequences)
    entering = first_in
    for phase in range(sections):
        if phase:
            received = [None, None]
            for side in (1, 0):
                received[side] = along(leaving[side], 1)
            entering = [
                jnp.where(section == 0, leaf, moved) for leaf, moved in zip(first_in, received)
            ]
        kept = layer_forward(entering)
        if phase + 1 < sections:
            leaving, feeds = layer_feed(kept, ())
    last_grad = split(top_grad)
    upstream = last_grad
    feeds = None
    sent = ()
    for phase in range(sections):
        if phase:
            sent = [low(leaf) for leaf in input_grads]
            received = [along(leaf, -1) for leaf in sent]
            upstream = [
                jnp.where(section == sections - 1, leaf, moved)
                for leaf, moved in zip(last_grad, received)
            ]
        if phase + 1 == sections:
            leaving, feeds = layer_feed(kept, sent)
        input_grads, vectors, triples, branch_grads, scatters = layer_backward(
            upstream, kept, feeds
        )
    activations = hand_back(merge(leaving))[None]

    down, up = scatters.down, scatters.up
    triple = starts_scatter(turned_product(kept.normed, triples, 768, True), False)
    out = starts_scatter(turned_product(branch_grads, kept.mixes, 256, True), True)
    vectors = low(vectors)
    halved = (vectors[..., :local_width], vectors[..., local_width:])
    mine = jnp.where(part == 0, halved[0], halved[1])
    theirs = swap(jnp.where(part == 0, halved[1], halved[0]))
    cores = jnp.where(part == 0, jnp.stack([mine, theirs]), jnp.stack([theirs, mine]))
    found = {0: cores}
    run(down.end_cross)
    run(up.beside, up.end_cross)
    hop(cores, pair_inner, PAIR_LINK, found, 1)
    triple.first[7] = tied(triple.first[7], up.got, BESIDE)
    triple.first[3] = tied(triple.first[3], down.got, CROSSED)
    run(triple.far_pair, triple.near_other, triple.end_pair, triple.end_cross)
    run(out.far_pair, out.near_pair)
    hop(found[0], across, ACROSS_LINK, found, 6)
    hop(found[1], across, ACROSS_LINK, found, 7)
    run(triple.far, triple.near, triple.beside)
    hop(jnp.stack([found[k] for k in (0, 1, 6, 7)]), outward, END_LINK, found, ENDED)
    out.first[3] = tied(out.first[3], up.got, CROSSED)
    run(out.end_pair, out.end_cross)
    input_gradient = hand_back(merge(input_grads), END_LINK, low)[None]
    run(triple.end_sum)
    out.got[FAR_PAIR] = tied(out.got[FAR_PAIR], triple.got, BESIDE)
    run(out.far, out.near, out.beside, out.end_sum)
    base = jnp.where(is_inner, rank, rank ^ 2)
    every = jnp.zeros((BOX,) + cores.shape, cores.dtype)
    for index, k in enumerate((0, 1, 6, 7)):
        entry = jnp.where(is_inner, found[k], found[ENDED][index])[None]
        every = lax.dynamic_update_slice_in_dim(every, entry, (base ^ k) % BOX, 0)
    if boxes > 1:
        every = lax.all_gather(every, "dp", axis=0, tiled=True, axis_index_groups=box_groups)
    adapt_every = jnp.concatenate(
        [every[r, 0] if r in inner else every[r ^ 2, 1] for r in range(ranks)], 0
    )
    modulation_gradient = jnp.einsum(
        "nr,nskc->srkc", scaled_rows, adapt_every, preferred_element_type=jnp.float32
    )[None]
    cond_rows_grad = jnp.einsum(
        "nskc,sdkc->nd", adapt_every, modulation_weight[0], preferred_element_type=jnp.float32
    )
    cond_rows_grad = tied(cond_rows_grad, out.got, MINE)
    cond_rows_grad = cond_rows_grad + swap(cond_rows_grad)
    section_grad = cond_rows_grad
    for steps in range(1, sections):
        turned = [(s, (s + steps) % sections) for s in range(sections)]
        section_grad = section_grad + lax.ppermute(cond_rows_grad, "section", turned)
    cond_grad = spread_small(silu_slope(cond_rows) * section_grad, 1)
    down_gradient = down.result()[None]
    up_gradient = up.result()[None]
    columns = width // (sections * parts * ranks)
    first_column = ((section * parts + part) * ranks + rank) * columns
    table_gradient = jnp.dot(
        wide(onehot_all).T,
        lax.dynamic_slice_in_dim(cond_grad, first_column, columns, 1),
        precision=lax.Precision.HIGHEST,
    )
    output_gradient = out.result()[None]
    projection_gradient = triple.result().reshape(2, rows, 3, local_width)[None]
    return (
        activations,
        input_gradient,
        table_gradient,
        modulation_gradient,
        projection_gradient,
        output_gradient,
        up_gradient,
        down_gradient,
    )


def solution(mesh):
    in_specs = (
        P("dp", None, None),
        P("dp", None, None),
        P("dp"),
        P("dp"),
        P(),
        P("section", None, "dp", None, "tensor"),
        P("section", None, "dp", None, "tensor"),
        P("section", None, "dp", "tensor"),
        P("section", None, "dp", "tensor"),
        P("section", None, "dp", "tensor"),
    )
    out_specs = (
        P("section", "dp", None, None),
        P("section", "dp", None, None),
        P(None, ("section", "tensor", "dp")),
        P("section", None, "dp", None, "tensor"),
        P("section", None, "dp", None, "tensor"),
        P("section", None, "dp", "tensor"),
        P("section", None, "dp", "tensor"),
        P("section", None, "dp", "tensor"),
    )
    return jax.shard_map(
        on_device, mesh=mesh, in_specs=in_specs, out_specs=out_specs, check_vma=False
    )
```

```python
import functools
from types import SimpleNamespace

import jax
import jax.numpy as jnp
from jax import lax
from jax.experimental import pallas as pl
from jax.experimental.pallas import tpu as pltpu
from jax.sharding import PartitionSpec as P

HEAD = 64
IMG = 128
BOX = 8
(FAR_PAIR, NEAR_PAIR, END, MINE, THEIRS, BESIDE, END_SUM, END_PAIR, CROSSED) = range(100, 109)
(PAIR_IN, END_IN, ACROSS_IN, PAIR_LINK, END_LINK, ACROSS_LINK, ENDED) = range(109, 116)
VMEM_LIMIT = 40 * 1024 * 1024


def norm_rows(values):
    centre = jnp.mean(values, axis=-1, keepdims=True)
    spread = values - centre
    variance = jnp.mean(spread * spread, axis=-1, keepdims=True)
    return spread * lax.rsqrt(variance + 1e-06)


def gelu_tanh(values):
    inner = 0.7978845608028654 * (values + 0.044715 * values * values * values)
    return 0.5 * values * (1.0 + jnp.tanh(inner))


def gelu_slope(values):
    square = values * values
    bend = jnp.tanh(0.7978845608028654 * (values + 0.044715 * values * square))
    return 0.5 * (1.0 + bend) + 0.5 * values * (1.0 - bend * bend) * (
        0.7978845608028654 * (1.0 + 0.134145 * square)
    )


def silu_slope(values):
    sigma = jax.nn.sigmoid(values)
    return sigma * (1.0 + values * (1.0 - sigma))


def left_dot(left, weight):
    return lax.dot_general(
        left, weight, (((1,), (0,)), ((), ())), preferred_element_type=jnp.float32
    )


def right_dot(left, weight):
    return lax.dot_general(
        left, weight, (((1,), (1,)), ((), ())), preferred_element_type=jnp.float32
    )


def rows_dot(left, right):
    return lax.dot_general(
        left, right, (((0,), (0,)), ((), ())), preferred_element_type=jnp.float32
    )


def flat(leaf):
    return leaf.reshape(-1, leaf.shape[-1])


def low(leaf):
    return leaf.astype(jnp.bfloat16)


def wide(leaf):
    return leaf.astype(jnp.float32)


def pair_mask(rows, half):
    lanes = lax.broadcasted_iota(jnp.int32, (rows, 2 * HEAD), 1)
    return lanes < HEAD if half == 0 else lanes >= HEAD


def only_half(leaf, half):
    return jnp.where(pair_mask(leaf.shape[0], half), leaf, jnp.zeros_like(leaf))


def stacked_rows(refs, column):
    lanes = pl.ds(column, 2 * HEAD)
    return jnp.concatenate([ref[:, lanes] for ref in refs], 0)


def put_rows(refs, column, value):
    start = 0
    for ref in refs:
        stop = start + ref.shape[0]
        ref[:, pl.ds(column, 2 * HEAD)] = value[start:stop]
        start = stop


def attention_kernel(counts, image, text, mixed_image, mixed_text):
    width = mixed_image.shape[1]
    total = image.shape[0] + text.shape[0]
    bound = IMG + counts[pl.program_id(0)]
    live = lax.broadcasted_iota(jnp.int32, (2 * total, total), 1) < bound
    for column in range(0, width, 2 * HEAD):
        queries = stacked_rows((image, text), column) * HEAD ** (-0.5)
        keys = stacked_rows((image, text), width + column)
        values = stacked_rows((image, text), 2 * width + column)
        asked = jnp.concatenate([only_half(queries, half) for half in range(2)], 0)
        scores = jnp.where(live, right_dot(asked, keys), -1e30)
        weights = jnp.exp(scores - jnp.max(scores, axis=-1, keepdims=True))
        share = 1.0 / jnp.sum(weights, axis=-1, keepdims=True)
        mixed = left_dot(low(weights), values) * share
        mixed = low(jnp.where(pair_mask(total, 0), mixed[:total], mixed[total:]))
        put_rows((mixed_image, mixed_text), column, mixed)


def attention_back_kernel(
    counts, image, text, grad_image, grad_text, out_image, out_text
):
    width = grad_image.shape[1]
    total = image.shape[0] + text.shape[0]
    bound = IMG + counts[pl.program_id(0)]
    live = lax.broadcasted_iota(jnp.int32, (total, 2 * total), 0) < bound
    scale = HEAD ** (-0.5)
    for column in range(0, width, 2 * HEAD):
        queries = stacked_rows((image, text), column) * scale
        keys = stacked_rows((image, text), width + column)
        values = stacked_rows((image, text), 2 * width + column)
        grads = stacked_rows((grad_image, grad_text), column)
        asked = jnp.concatenate([only_half(queries, half) for half in range(2)], 0)
        given = jnp.concatenate([only_half(grads, half) for half in range(2)], 0)
        scores = jnp.where(live, right_dot(keys, asked), -1e30)
        soft = jnp.exp(scores - jnp.max(scores, axis=0, keepdims=True))
        soft = soft * (1.0 / jnp.sum(soft, axis=0, keepdims=True))
        prob_grad = right_dot(values, given)
        drop = jnp.sum(prob_grad * soft, axis=0, keepdims=True)
        score_grad = low(soft * (prob_grad - drop))
        query_grad = rows_dot(score_grad, keys) * scale
        query_grad = jnp.where(pair_mask(total, 0), query_grad[:total], query_grad[total:])
        refs = (out_image, out_text)
        put_rows(refs, column, low(query_grad))
        put_rows(refs, width + column, low(left_dot(score_grad, asked)))
        put_rows(refs, 2 * width + column, low(left_dot(low(soft), given)))


def by_sequence_call(kernel, counts, inputs, widths, name, matmuls, light):
    group = counts.shape[0]

    def spec(rows, width):
        return pl.BlockSpec((rows, width), lambda n, counts: (n, 0))

    rows = [leaf.shape[0] // group for leaf in inputs[:2]]
    total = sum(rows)
    return pl.pallas_call(
        kernel,
        grid_spec=pltpu.PrefetchScalarGridSpec(
            num_scalar_prefetch=1,
            grid=(group,),
            in_specs=[spec(leaf.shape[0] // group, leaf.shape[1]) for leaf in inputs],
            out_specs=[spec(count, widths) for count in rows],
        ),
        out_shape=[
            jax.ShapeDtypeStruct((group * count, widths), jnp.bfloat16) for count in rows
        ],
        compiler_params=pltpu.CompilerParams(vmem_limit_bytes=48 * 1024 * 1024),
        cost_estimate=estimate(
            7 * matmuls * group * total * total * 12 * 2 * HEAD,
            sum(leaf.size for leaf in inputs) + group * total * widths,
            light,
        ),
        name=name,
    )(counts, *inputs)


def attention(counts, packed, heads):
    return by_sequence_call(
        attention_kernel, counts, list(packed), heads * HEAD, "attention", 2, False
    )


def attention_back(counts, packed, grads, heads, light):
    return by_sequence_call(
        attention_back_kernel,
        counts,
        list(packed) + list(grads),
        3 * heads * HEAD,
        "attention_back",
        5,
        light,
    )


def joined_rows(refs):
    values = [ref[...] for ref in refs]
    return values[0] if len(values) == 1 else jnp.concatenate(values, 0)


def store_rows(refs, value):
    start = 0
    for ref in refs:
        stop = start + ref.shape[0]
        ref[...] = value[start:stop].astype(ref.dtype)
        start = stop


def product_kernel(counts, dims, finish, *refs):
    lefts, extras, outs = counts
    right = refs[lefts][...]
    total = lax.dot_general(
        joined_rows(refs[:lefts]), right, (dims, ((), ())), preferred_element_type=jnp.float32
    )
    refs = refs[lefts + 1 :]
    results = finish(total, *[ref[...] for ref in refs[:extras]])
    refs = refs[extras:]
    for count, value in zip(outs, results):
        store_rows(refs[:count], value)
        refs = refs[count:]


def turned_kernel(lefts, tiles, *refs):
    turned = refs[-len(lefts) :]
    result = refs[-len(lefts) - 1]
    step = pl.program_id(0)
    start = 0
    for side, count in enumerate(lefts):
        sources = refs[start : start + count]
        right = refs[start + count]
        start += count + 1

        @pl.when(step == side * tiles)
        def _(sources=sources, held=turned[side]):
            held[...] = joined_rows(sources).T

        @pl.when(jnp.logical_and(step >= side * tiles, step < (side + 1) * tiles))
        def _(right=right, held=turned[side]):
            result[...] = low(left_dot(held[...], right[...]))


def estimate(flops, values, light):
    return pl.CostEstimate(flops=2 * flops, bytes_accessed=2 * values, transcendentals=0)


def product(lefts, right, side, turned, tile, outs, light, finish=None, extras=()):
    depth = lefts[0].shape[1]
    width = right.shape[1] if turned else right.shape[2]
    if turned:
        right_spec = pl.BlockSpec((None, tile, depth), lambda n: (side, n, 0))
    else:
        right_spec = pl.BlockSpec((None, depth, tile), lambda n: (side, 0, n))
    rows = sum(leaf.shape[0] for leaf in lefts)
    counts = [count for group in outs for count in group]
    kernel = functools.partial(
        product_kernel,
        (len(lefts), len(extras), [len(group) for group in outs]),
        ((1,), (1 if turned else 0,)),
        finish or (lambda total: (total,)),
    )
    return pl.pallas_call(
        kernel,
        grid=(width // tile,),
        in_specs=[pl.BlockSpec(leaf.shape, lambda n: (0, 0)) for leaf in lefts]
        + [right_spec]
        + [pl.BlockSpec((rows, tile), lambda n: (0, n)) for leaf in extras],
        out_specs=[pl.BlockSpec((count, tile), lambda n: (0, n)) for count in counts],
        out_shape=[jax.ShapeDtypeStruct((count, width), jnp.bfloat16) for count in counts],
        compiler_params=pltpu.CompilerParams(vmem_limit_bytes=VMEM_LIMIT),
        cost_estimate=estimate(2 * rows * depth * width, depth * width + 2 * rows * width, light),
    )(*lefts, right, *extras)


def turned_product(lefts, rights, tile, light):
    depth, width = lefts[0][0].shape[1], rights[0].shape[1]
    tiles = width // tile
    in_specs, operands, scratch = ([], [], [])
    for side, (left, right) in enumerate(zip(lefts, rights)):
        first = side * tiles
        in_specs += [pl.BlockSpec(leaf.shape, lambda n: (0, 0)) for leaf in left]
        in_specs.append(
            pl.BlockSpec(
                (right.shape[0], tile), lambda n, first=first: (0, jnp.clip(n - first, 0, tiles - 1))
            )
        )
        operands += list(left) + [right]
        scratch.append(pltpu.VMEM((depth, right.shape[0]), jnp.bfloat16))
    rows = sum(right.shape[0] for right in rights)
    return pl.pallas_call(
        functools.partial(turned_kernel, [len(left) for left in lefts], tiles),
        grid=(len(lefts) * tiles,),
        in_specs=in_specs,
        out_specs=pl.BlockSpec((None, depth, tile), lambda n: (n // tiles, 0, n % tiles)),
        out_shape=jax.ShapeDtypeStruct((len(lefts), depth, width), jnp.bfloat16),
        scratch_shapes=scratch,
        compiler_params=pltpu.CompilerParams(vmem_limit_bytes=VMEM_LIMIT),
        cost_estimate=estimate(2 * rows * depth * width, depth * width, light),
    )(*operands)


def with_gelu(before):
    return before, gelu_tanh(before)


def times_slope(after_grad, before):
    return (after_grad * gelu_slope(wide(before)),)


def on_device(
    tokens,
    cotangent,
    times,
    text_counts,
    time_table,
    modulation_weight,
    projection_weight,
    output_weight,
    up_weight,
    down_weight,
):
    micro, length, width = tokens.shape
    sections = lax.axis_size("section")
    section = lax.axis_index("section")
    parts = lax.axis_size("tensor")
    part = lax.axis_index("tensor")
    ranks = lax.axis_size("dp")
    rank = lax.axis_index("dp")
    local_width = projection_weight.shape[4]
    rows = projection_weight.shape[2]

    inner = [r for r in range(ranks) if (r >> 1) % 4 in (1, 2)]
    outer = [r for r in range(ranks) if (r >> 1) % 4 in (0, 3)]
    is_inner = jnp.logical_or((rank >> 1) % 4 == 1, (rank >> 1) % 4 == 2)
    pair_all = [(r, r ^ 1) for r in range(ranks)]
    pair_inner = [(r, r ^ 1) for r in inner]
    pair_outer = [(r, r ^ 1) for r in outer]
    inward = [(r, r ^ 2) for r in outer]
    outward = [(r, r ^ 2) for r in inner]
    across = [(r, r ^ 6) for r in inner]
    boxes = ranks // BOX
    box_groups = [[b * BOX + i for b in range(boxes)] for i in range(BOX)]

    links = {}
    depths = {}

    def tied(value, holder, name):
        value, holder[name] = lax.optimization_barrier((value, holder[name]))
        return value

    def hop(value, pairs, link=None, holder=None, name=0, axis="dp"):
        queue = links.setdefault(link, [])
        depth = depths.get(link, 1)
        if link is not None and len(queue) >= depth:
            value = tied(value, *queue[-depth])
        moved = lax.ppermute(value, axis, pairs)
        holder = {} if holder is None else holder
        holder[name] = moved
        if link is not None:
            queue.append((holder, name))
        return moved

    def by_bits(bit):
        return [(r, r ^ bit) for r in range(ranks)]

    def spread_small(value, axis, queued=False, gates=()):
        bit = 1
        gates = list(gates)
        while bit < ranks:
            link = {1: PAIR_LINK, 2: END_LINK, 4: ACROSS_LINK}.get(bit) if queued else None
            if bit > 1 and gates:
                value, _ = lax.optimization_barrier((value, gates.pop(0)))
            other = hop(value, by_bits(bit), link)
            value = jnp.where(
                (rank & bit) == 0,
                jnp.concatenate([value, other], axis),
                jnp.concatenate([other, value], axis),
            )
            bit *= 2
        return value

    def swap(value):
        return lax.ppermute(value, "tensor", [(p, p ^ 1) for p in range(parts)])

    def along(value, steps):
        first, last = (max(0, -steps), min(sections, sections - steps))
        return lax.ppermute(value, "section", [(s, s + steps) for s in range(first, last)])

    def place(step):
        return (rank ^ step) % BOX

    def gather_all(arrays, later):
        pieces = [{0: own} for own, heavy in arrays]
        heavies = [heavy for own, heavy in arrays]
        count = len(arrays)

        def step(index, target, source, pairs, link):
            if 0 <= index < count:
                hop(pieces[index][source], pairs, link, pieces[index], target)

        step(0, 1, 0, pair_all, PAIR_IN)
        step(0, 2, 0, inward, END_IN)
        step(0, 6, 0, across, ACROSS_IN)
        for index in range(count):
            step(index + 1, 1, 0, pair_all, PAIR_IN)
            step(index, 3, 1, inward, END_IN)
            step(index, 4, 2, across, ACROSS_IN)
            if heavies[index]:
                step(index, 7, 6, pair_inner, PAIR_IN)
            else:
                step(index, 7, 1, across, ACROSS_IN)
            step(index + 1, 2, 0, inward, END_IN)
            step(index + 1, 6, 0, across, ACROSS_IN)
            step(index, 5, 4, pair_inner, PAIR_IN)
        later, pieces[1][2] = lax.optimization_barrier((later, pieces[1][2]))
        wholes = []
        for found in pieces:
            own = found[0]
            shape = (own.shape[0], BOX, rows, own.shape[2])
            whole = jnp.broadcast_to(found[1][0, 0, 0], shape)
            for at, piece in found.items():
                whole = lax.dynamic_update_slice_in_dim(whole, piece[:, None], place(at), 1)
            whole = whole.reshape(shape[0], BOX * rows, shape[3])
            if boxes > 1:
                whole = lax.all_gather(
                    whole, "dp", axis=1, tiled=True, axis_index_groups=box_groups
                )
            wholes.append(whole)
        arrivals = [pieces[0][2], pieces[0][6], pieces[1][6], pieces[3][6]]
        return wholes, (later, arrivals)

    def starts_scatter(pair, pair_heavy):
        if boxes > 1:
            pair = lax.psum_scatter(
                pair, "dp", scatter_dimension=1, tiled=True, axis_index_groups=box_groups
            )

        apart_rows = pair.reshape(pair.shape[0], BOX, rows, pair.shape[2])

        def block(step, source=apart_rows):
            return lax.dynamic_index_in_dim(source, place(step), 1, False)

        def plus(step, name):
            source = tied(apart_rows, got, name)
            return low(wide(block(step, source)) + wide(got[name]))

        got = {}
        first = {step: block(step) for step in (3, 5, 7)}

        def gated_by_first(values):
            values, held = lax.optimization_barrier((values, first))
            first.update(held)
            return values

        def far_pair():
            hop(first[5], pair_inner, PAIR_LINK, got, FAR_PAIR)

        def near_pair():
            hop(first[7], pair_inner, PAIR_LINK, got, NEAR_PAIR)

        def far():
            hop(plus(4, FAR_PAIR), across, ACROSS_LINK, got, END)

        def near():
            near = plus(6, NEAR_PAIR) if pair_heavy else block(6)
            hop(near, across, ACROSS_LINK, got, MINE)

        def near_other():
            hop(first[7], across, ACROSS_LINK, got, THEIRS)

        def beside():
            own = block(1) if pair_heavy else plus(1, THEIRS)
            hop(own, pair_inner, PAIR_LINK, got, BESIDE)

        def end_pair():
            hop(first[3], outward, END_LINK, got, END_PAIR)

        def end_cross():
            hop(got[END_PAIR], pair_outer, None, got, CROSSED)

        def end_sum():
            hop(plus(2, END), outward, END_LINK, got, END_SUM)

        def result():
            inner_sum = wide(block(0)) + wide(got[MINE]) + wide(got[BESIDE])
            end_total = wide(got[END_SUM]) + wide(got[CROSSED])
            return jnp.where(is_inner, inner_sum, end_total)

        return SimpleNamespace(
            got=got,
            gate=gated_by_first,
            far_pair=far_pair,
            near_pair=near_pair,
            far=far,
            near=near,
            near_other=near_other,
            beside=beside,
            end_pair=end_pair,
            end_cross=end_cross,
            first=first,
            end_sum=end_sum,
            result=result,
        )

    def run(*steps):
        for step in steps:
            step()

    def two_core(pairs):
        return [(ranks + source, ranks + target) for source, target in pairs]

    def take_in(value):
        moved = lax.ppermute(value, ("tensor", "dp"), two_core(inward))
        return jnp.where(part == 0, value, moved)

    def hand_back(value, link=None, narrow=lambda leaf: leaf):
        moved = hop(narrow(value), two_core(outward), link, axis=("tensor", "dp")).astype(value.dtype)
        held = jnp.where(is_inner, value, moved)
        return jnp.where((part == 0) == is_inner, held, swap(held))

    own_rank = rank ^ (2 * part)
    other_rank = rank ^ (2 * (1 - part))
    (out_matrix, triple_matrix, up_matrix, down_matrix), held = gather_all(
        [
            (output_weight[0], True),
            (projection_weight[0].reshape(2, rows, 3 * local_width), False),
            (up_weight[0], True),
            (down_weight[0], False),
        ],
        tokens,
    )
    own_rank = rank ^ (2 * part)
    other_rank = rank ^ (2 * (1 - part))
    (out_matrix, triple_matrix, up_matrix, down_matrix), held = gather_all(
        [
            (output_weight[0], True),
            (projection_weight[0].reshape(2, rows, 3 * local_width), False),
            (up_weight[0], True),
            (down_weight[0], False),
        ],
        tokens,
    )
    tokens, arrivals = held
    both_all = spread_small(jnp.stack([times, text_counts]), 1, gates=arrivals[:2])
    both_all, arrivals[2] = lax.optimization_barrier((both_all, arrivals[2]))
    times_all, counts_all = both_all[0], both_all[1]
    sequences = take_in(tokens)
    top_grad = take_in(cotangent)

    onehot_all = (times_all[:, None] == jnp.arange(time_table.shape[0])[None, :]).astype(
        jnp.bfloat16
    )
    cond_all = jnp.dot(onehot_all, time_table, preferred_element_type=jnp.float32)
    cond_rows = lax.dynamic_slice_in_dim(cond_all, rank * rows, rows, 1)
    scaled_rows = jax.nn.silu(cond_rows).astype(jnp.bfloat16)
    adapt_part = jnp.einsum(
        "nd,sdkc->nskc", scaled_rows, modulation_weight[0], preferred_element_type=jnp.float32
    )

    def of_rank(stacked, index):
        return lax.dynamic_slice_in_dim(stacked, index * micro, micro, 0)

    def joined(mine, theirs, axis):
        return jnp.where(
            part == 0,
            jnp.concatenate([mine, theirs], axis),
            jnp.concatenate([theirs, mine], axis),
        )

    def pair_of_rank(index):
        return jnp.stack([of_rank(adapt_part, index), of_rank(adapt_part, index ^ 2)])

    adapt_terms = [pair_of_rank(rank)]
    for bit in range(1, ranks):
        pairs = [(r, r ^ bit) for r in range(ranks) if r ^ bit in inner]
        adapt_terms.append(hop(pair_of_rank(rank ^ bit), pairs))
    adapt_terms, arrivals[3] = lax.optimization_barrier((adapt_terms, arrivals[3]))
    adapt_pair = sum(adapt_terms)
    adapt_mine = jnp.where(part == 0, adapt_pair[0], adapt_pair[1])
    adapt_other = swap(jnp.where(part == 0, adapt_pair[1], adapt_pair[0]))
    adapt = joined(adapt_mine, adapt_other, 3)
    counts = jnp.concatenate([of_rank(counts_all, own_rank), of_rank(counts_all, other_rank)])
    group = parts * micro
    text_rows = -(-(length - IMG) // 16) * 16
    heads = local_width // HEAD

    def both(own):
        return [own, swap(own)]

    def own_total(partial):
        return wide(partial[0]) + wide(swap(partial[1]))

    def halves(like):
        return [leaf.shape[0] for leaf in like]

    def split(leaf):
        text = jnp.pad(leaf[:, IMG:], ((0, 0), (0, text_rows - (length - IMG)), (0, 0)))
        return [flat(leaf[:, :IMG]), flat(text)]

    def merge(sides):
        image, text = (leaf.reshape(micro, -1, width) for leaf in sides)
        return jnp.concatenate([image, text[:, : length - IMG]], 1)

    def by_sequence(leaf):
        return jnp.sum(leaf.reshape(micro, -1, leaf.shape[-1]), axis=1)

    def vector_of(side, index):
        return adapt[:, side, index][:, None]

    def apart(leaf):
        return leaf.reshape(micro, -1, leaf.shape[-1])

    def modulated(values, side, first):
        values = apart(values)
        result = norm_rows(values) * (1.0 + vector_of(side, first + 1))
        return flat(low(result + vector_of(side, first)))

    def gated(values, side, index):
        return flat(apart(values) * vector_of(side, index))

    def norm_back(values, grad, side, first):
        values, grad = (apart(values), apart(grad))
        centre = jnp.mean(values, axis=-1, keepdims=True)
        spread = values - centre
        variance = jnp.mean(spread * spread, axis=-1, keepdims=True)
        inverse = lax.rsqrt(variance + 1e-06)
        unit = spread * inverse
        inner_grad = grad * (1.0 + vector_of(side, first + 1))
        tilt = jnp.mean(inner_grad * unit, axis=-1, keepdims=True)
        level = jnp.mean(inner_grad, axis=-1, keepdims=True)
        result = inverse * (inner_grad - level - unit * tilt)
        return flat(result), jnp.sum(grad * unit, axis=1), jnp.sum(grad, axis=1)

    def layer_forward(sides):
        normed = [both(modulated(wide(sides[side]), side, 0)) for side in range(2)]
        packed = [
            product(
                normed[side], triple_matrix, side, False, 768, [[sum(halves(normed[side]))]], False
            )[0]
            for side in range(2)
        ]
        mixes = attention(counts, packed, heads)
        kept = SimpleNamespace(sides=sides, normed=normed, packed=packed, mixes=mixes)
        kept.branch, kept.middles, kept.seconds, kept.befores, kept.afters = ([], [], [], [], [])
        for side in range(2):
            branch = own_total(
                product([mixes[side]], out_matrix, side, True, 512, [halves(normed[side])], False)
            )
            middle = wide(sides[side]) + gated(branch, side, 2)
            kept.branch.append(branch)
            kept.middles.append(middle)
            kept.seconds.append(both(modulated(middle, side, 3)))
        for side in range(2):
            second = kept.seconds[side]
            rows_all = [sum(halves(second))]
            before, after = product(
                second, up_matrix, side, False, 1024, [rows_all, rows_all], False, with_gelu
            )
            kept.befores.append(before)
            kept.afters.append(after)
        return kept

    def layer_feed(kept, gate):
        afters, gate = lax.optimization_barrier((kept.afters, gate))
        results = [None, None]
        feeds = [None, None]
        for side in (1, 0):
            partial = product(
                [afters[side]], down_matrix, side, True, 512, [halves(kept.seconds[side])], False
            )
            feeds[side] = own_total(partial)
            if side == 1:
                feeds[1], afters[0] = lax.optimization_barrier((feeds[1], afters[0]))
            results[side] = low(kept.middles[side] + gated(feeds[side], side, 5))
        return results, feeds

    def layer_backward(incoming, kept, feeds):
        final = feeds is not None
        up_grads, middle_grads, branch_grads, mix_grads = ([], [], [], [])
        vectors = [[None] * 6, [None] * 6]
        feed_grads = [both(low(gated(wide(incoming[side]), side, 5))) for side in range(2)]
        scatters = SimpleNamespace()
        if final:
            down = starts_scatter(turned_product(feed_grads, kept.afters, 512, True), False)
            feed_grads = down.gate(feed_grads)
            run(down.far_pair, down.near_other, down.near, down.end_pair)
            feed_grads[1] = tied(feed_grads[1], down.got, THEIRS)
            scatters.down = down
        for side in range(2):
            feed_grad = feed_grads[side]
            rows_all = [[sum(halves(feed_grad))]]
            up_grad = product(
                feed_grad,
                down_matrix,
                side,
                False,
                1024,
                rows_all,
                final,
                times_slope,
                [kept.befores[side]],
            )[0]
            up_grads.append(up_grad)
        if final:
            up_gradient = turned_product(kept.seconds, up_grads, 512, True)
        second_parts = [
            product([up_grads[side]], up_matrix, side, True, 512, [halves(feed_grads[side])], final)
            for side in range(2)
        ]
        if final:
            up = starts_scatter(up_gradient, True)
            scatters.up = up
            run(up.far_pair, up.near_pair, up.end_pair)
            run(down.far)
            run(up.far)
            run(down.beside)
            run(up.near)
        for side in range(2):
            upstream = wide(incoming[side])
            feed_grad = feed_grads[side]
            up_grad = up_grads[side]
            rows_all = [[sum(halves(feed_grad))]]
            if final:
                vectors[side][5] = by_sequence(upstream * feeds[side])
            else:
                vectors[side][5] = jnp.zeros((micro, width), jnp.float32)
            second_grad = own_total(second_parts[side])
            middle_part, vectors[side][4], vectors[side][3] = norm_back(
                kept.middles[side], second_grad, side, 3
            )
            middle_grad = upstream + middle_part
            branch_grad = both(low(gated(middle_grad, side, 2)))
            middle_grads.append(middle_grad)
            branch_grads.append(branch_grad)
            vectors[side][2] = by_sequence(middle_grad * kept.branch[side])
            mix_grads.append(
                product(branch_grad, out_matrix, side, False, 256, rows_all, final)[0]
            )
        triples = list(attention_back(counts, kept.packed, mix_grads, heads, final))
        if final:
            run(down.end_sum)
            run(up.end_sum)
        results = []
        partials = []
        for side in range(2):
            partials.append(
                product(
                    [triples[side]],
                    triple_matrix,
                    side,
                    True,
                    512,
                    [halves(branch_grads[side])],
                    final,
                )
            )
        for side in range(2):
            first_grad = own_total(partials[side])
            input_part, vectors[side][1], vectors[side][0] = norm_back(
                wide(kept.sides[side]), first_grad, side, 0
            )
            results.append(middle_grads[side] + input_part)
        vectors = jnp.stack([jnp.stack(v, 1) for v in vectors], 1)
        return (results, vectors, triples, branch_grads, scatters)

    first_in = split(sequences)
    entering = first_in
    for phase in range(sections):
        if phase:
            received = [None, None]
            for side in (1, 0):
                received[side] = along(leaving[side], 1)
            entering = [
                jnp.where(section == 0, leaf, moved) for leaf, moved in zip(first_in, received)
            ]
        kept = layer_forward(entering)
        if phase + 1 < sections:
            leaving, feeds = layer_feed(kept, ())
    last_grad = split(top_grad)
    upstream = last_grad
    feeds = None
    sent = ()
    for phase in range(sections):
        if phase:
            sent = [low(leaf) for leaf in input_grads]
            received = [along(leaf, -1) for leaf in sent]
            upstream = [
                jnp.where(section == sections - 1, leaf, moved)
                for leaf, moved in zip(last_grad, received)
            ]
        if phase + 1 == sections:
            leaving, feeds = layer_feed(kept, sent)
        input_grads, vectors, triples, branch_grads, scatters = layer_backward(
            upstream, kept, feeds
        )
    activations = hand_back(merge(leaving))[None]

    down, up = scatters.down, scatters.up
    triple = starts_scatter(turned_product(kept.normed, triples, 768, True), False)
    out = starts_scatter(turned_product(branch_grads, kept.mixes, 256, True), True)
    vectors = low(vectors)
    halved = (vectors[..., :local_width], vectors[..., local_width:])
    mine = jnp.where(part == 0, halved[0], halved[1])
    theirs = swap(jnp.where(part == 0, halved[1], halved[0]))
    cores = jnp.where(part == 0, jnp.stack([mine, theirs]), jnp.stack([theirs, mine]))
    found = {0: cores}
    run(down.end_cross)
    run(up.beside, up.end_cross)
    hop(cores, pair_inner, PAIR_LINK, found, 1)
    triple.first[7] = tied(triple.first[7], up.got, BESIDE)
    triple.first[3] = tied(triple.first[3], down.got, CROSSED)
    run(triple.far_pair, triple.near_other, triple.end_pair, triple.end_cross)
    run(out.far_pair, out.near_pair)
    hop(found[0], across, ACROSS_LINK, found, 6)
    hop(found[1], across, ACROSS_LINK, found, 7)
    run(triple.far, triple.near, triple.beside)
    hop(jnp.stack([found[k] for k in (0, 1, 6, 7)]), outward, END_LINK, found, ENDED)
    out.first[3] = tied(out.first[3], up.got, CROSSED)
    run(out.end_pair, out.end_cross)
    input_gradient = hand_back(merge(input_grads), END_LINK, low)[None]
    run(triple.end_sum)
    out.got[FAR_PAIR] = tied(out.got[FAR_PAIR], triple.got, BESIDE)
    run(out.far, out.near, out.beside, out.end_sum)
    base = jnp.where(is_inner, rank, rank ^ 2)
    every = jnp.zeros((BOX,) + cores.shape, cores.dtype)
    for index, k in enumerate((0, 1, 6, 7)):
        entry = jnp.where(is_inner, found[k], found[ENDED][index])[None]
        every = lax.dynamic_update_slice_in_dim(every, entry, (base ^ k) % BOX, 0)
    if boxes > 1:
        every = lax.all_gather(every, "dp", axis=0, tiled=True, axis_index_groups=box_groups)
    adapt_every = jnp.concatenate(
        [every[r, 0] if r in inner else every[r ^ 2, 1] for r in range(ranks)], 0
    )
    modulation_gradient = jnp.einsum(
        "nr,nskc->srkc", scaled_rows, adapt_every, preferred_element_type=jnp.float32
    )[None]
    cond_rows_grad = jnp.einsum(
        "nskc,sdkc->nd", adapt_every, modulation_weight[0], preferred_element_type=jnp.float32
    )
    cond_rows_grad = tied(cond_rows_grad, out.got, MINE)
    cond_rows_grad = cond_rows_grad + swap(cond_rows_grad)
    section_grad = cond_rows_grad
    for steps in range(1, sections):
        turned = [(s, (s + steps) % sections) for s in range(sections)]
        section_grad = section_grad + lax.ppermute(cond_rows_grad, "section", turned)
    cond_grad = spread_small(silu_slope(cond_rows) * section_grad, 1)
    down_gradient = down.result()[None]
    up_gradient = up.result()[None]
    columns = width // (sections * parts * ranks)
    first_column = ((section * parts + part) * ranks + rank) * columns
    table_gradient = jnp.dot(
        wide(onehot_all).T,
        lax.dynamic_slice_in_dim(cond_grad, first_column, columns, 1),
        precision=lax.Precision.HIGHEST,
    )
    output_gradient = out.result()[None]
    projection_gradient = triple.result().reshape(2, rows, 3, local_width)[None]
    return (
        activations,
        input_gradient,
        table_gradient,
        modulation_gradient,
        projection_gradient,
        output_gradient,
        up_gradient,
        down_gradient,
    )


def solution(mesh):
    in_specs = (
        P("dp", None, None),
        P("dp", None, None),
        P("dp"),
        P("dp"),
        P(),
        P("section", None, "dp", None, "tensor"),
        P("section", None, "dp", None, "tensor"),
        P("section", None, "dp", "tensor"),
        P("section", None, "dp", "tensor"),
        P("section", None, "dp", "tensor"),
    )
    out_specs = (
        P("section", "dp", None, None),
        P("section", "dp", None, None),
        P(None, ("section", "tensor", "dp")),
        P("section", None, "dp", None, "tensor"),
        P("section", None, "dp", None, "tensor"),
        P("section", None, "dp", "tensor"),
        P("section", None, "dp", "tensor"),
        P("section", None, "dp", "tensor"),
    )
    return jax.shard_map(
        on_device, mesh=mesh, in_specs=in_specs, out_specs=out_specs, check_vma=False
    )
```
